32 devices in a mesh: dp: 2 (over x), seq: 16 (over z, y, core).
Axes of the slice: x: 2, y: 2, z: 4, core: 2. Of those that a mesh axis runs over, the one named last changes fastest.
Arguments:
- tokens: bfloat16 [8192, 512], P(('dp', 'seq')), parts along dimension 0, may hold values from -16 to 16
- globals_in: bfloat16 [256, 512], P('dp'), parts along dimension 0, may hold values from -16 to 16
- seg_ids: int32 [8192], P(('dp', 'seq')), parts along dimension 0, may hold values from 1 to 63, as said below
- global_table: int32 [256], P('dp'), parts along dimension 0, may hold values from 1 to 63
- w_qkv: bfloat16 [2, 512, 1536], replicated, may hold values from -1 to 1
- w_out: bfloat16 [2, 512, 512], replicated, may hold values from -0.25 to 0.25
- gain_local: float32 [2, 512], replicated, may hold values from 0.5 to 1.5
- gain_global: float32 [2, 512], replicated, may hold values from 0.5 to 1.5
- seg_bias: float32 [2, 8], replicated, may hold values from 2 to 5
Outputs:
- local_out: bfloat16 [8192, 512], P(('dp', 'seq')), parts along dimension 0
- global_out: bfloat16 [256, 512], P('dp'), parts along dimension 0
The draws below stay inside these ranges and needn't reach their ends.
There are 2 independent parts, one for each index of `dp`. The reference program is written for one: setup_inputs(seed, part) draws one part's arguments, and reference() takes and returns one part's arrays. A program takes and returns all parts, laid end to end along the dimension named above; an argument that names none is the same for every part. Nothing has to cross between parts.
Inputs may be any that keep to these rules, and one draw needn't show every extreme that they name: `seg_ids`: the entity ids come in runs of 128 consecutive tokens (the first and last runs of a context are shorter).
All inputs are finite; a program needn't handle non-finite values.
Results may differ from the reference program's by a relative error of at most 0.006.
Values may be sent and summed in bfloat16 or wider, within the bound.
A program may use at most 192 MiB of HBM per device.

```python
import math
import jax
import jax.numpy as jnp
from jax import lax

D = 512
H = 8
G = 128
RADIUS = 256
KEYS = 64
LAYERS = 2
TOK_DEV = 256
SEQ = 4096


def drawn_direction():
    phase = (jnp.arange(D, dtype=jnp.int32) * 37 % D).astype(jnp.float32)
    return math.sqrt(2.0) * jnp.cos(phase * (2.0 * math.pi / D) + 0.5)


def marked_rows(key, count, share):
    noise_key, mark_key, level_key = jax.random.split(key, 3)
    noise = jax.random.truncated_normal(noise_key, -6.0, 6.0, (count, D), jnp.float32)
    level = jax.random.uniform(level_key, (count, 1), jnp.float32, 1.5, 4.0)
    marked = jax.random.bernoulli(mark_key, share, (count, 1)).astype(jnp.float32)
    return noise + marked * level * drawn_direction()[None, :]


def draw_tokens(key, part):
    return marked_rows(jax.random.fold_in(key, 11), SEQ, 0.0625).astype(jnp.bfloat16)


def draw_globals_in(key, part):
    return marked_rows(jax.random.fold_in(key, 23), G, 0.25).astype(jnp.bfloat16)


def draw_seg_ids(key, part):
    run_length = max(RADIUS // 2, 1)
    run_count = SEQ // run_length + 1
    run_ids = jax.random.randint(jax.random.fold_in(key, 53), (run_count,), 1, KEYS, jnp.int32)
    which = (jnp.arange(SEQ, dtype=jnp.int32) + run_length // 2) // run_length
    return run_ids[which]


def draw_w_qkv(key, part):
    base_key = jax.random.fold_in(key, 37)
    base = jax.random.truncated_normal(base_key, -4.0, 4.0, (LAYERS, D, 3 * D), jnp.float32) / math.sqrt(D)
    head_size = D // H
    strength = math.sqrt(270.0 / math.sqrt(head_size))
    column = jnp.arange(D, dtype=jnp.int32)
    signs = jnp.where((column * 7 + column // 3) % 2 == 0, 1.0, -1.0).astype(jnp.float32)
    pattern = strength / D * drawn_direction()[:, None] * signs[None, :]
    plant = jnp.concatenate([pattern, pattern, jnp.zeros((D, D), jnp.float32)], axis=1)
    return (base + plant[None]).astype(jnp.bfloat16)


def with_ends(drawn, own_key, smallest, high):
    longest = drawn.shape.index(max(drawn.shape))
    spots = []
    for shift in (0, 1):
        where = [jax.random.randint(jax.random.fold_in(own_key, axis), (), 0, length) for axis, length in enumerate(drawn.shape)]
        where[longest] = (where[longest] + shift) % drawn.shape[longest]
        spots.append(tuple(where))
    return drawn.at[spots[0]].set(smallest).at[spots[1]].set(high)


def gaussian(own_key, shape, scale, reach, held_as=jnp.bfloat16):
    drawn = scale * jax.random.normal(own_key, shape, jnp.float32)
    return jnp.clip(drawn, min=-reach, max=reach).astype(held_as)


def setup_inputs(seed: int = 0, part: int = 0) -> dict:
    seeds = jax.random.split(jax.random.key(seed), 10)
    part_splits = jax.random.split(jax.random.fold_in(seeds[9], part), 10)
    tokens = draw_tokens(jax.random.fold_in(jax.random.fold_in(seeds[9], part), 71), part)
    globals_in = draw_globals_in(jax.random.fold_in(jax.random.fold_in(seeds[9], part), 71), part)
    seg_ids = draw_seg_ids(jax.random.fold_in(jax.random.fold_in(seeds[9], part), 71), part)
    global_table = with_ends(jax.random.randint(part_splits[3], (G,), 1, KEYS), jax.random.fold_in(part_splits[3], 1), 1, KEYS - 1).astype(jnp.int32)
    w_qkv = draw_w_qkv(jax.random.fold_in(seeds[9], 71), part)
    w_out = gaussian(seeds[5], (LAYERS, D, D), D ** -0.5, 0.25)
    gain_local = jnp.clip(1.0 + 0.1 * jax.random.normal(seeds[6], (LAYERS, D), jnp.float32), 0.5, 1.5)
    gain_global = jnp.clip(1.0 + 0.1 * jax.random.normal(seeds[7], (LAYERS, D), jnp.float32), 0.5, 1.5)
    seg_bias = jnp.clip(jax.random.uniform(seeds[8], (LAYERS, H), jnp.float32, 2.0, 5.0), 2.0, 5.0)
    return dict(tokens=tokens, globals_in=globals_in, seg_ids=seg_ids, global_table=global_table, w_qkv=w_qkv, w_out=w_out, gain_local=gain_local, gain_global=gain_global, seg_bias=seg_bias)


masked_fill = -1e+30

def layer_norm(values, gain):
    average = lax.optimization_barrier(jnp.mean(values, axis=-1, keepdims=True))
    centered = values - average
    variance = lax.optimization_barrier(jnp.mean(centered * centered, axis=-1, keepdims=True))
    return (centered * lax.rsqrt(variance + 1e-05) * gain).astype(jnp.bfloat16)

def window_attend(queries, keys_ext, values_ext, seg_rows, seg_ext, valid, gkeys, gvalues, bias, scaling):
    rows = queries.shape[0]
    span = keys_ext.shape[0]
    radius = (span - rows) // 2
    scores = jnp.einsum('thd,shd->hts', queries, keys_ext, preferred_element_type=jnp.float32) * scaling
    offset = jnp.arange(span, dtype=jnp.int32)[None, :] - radius - jnp.arange(rows, dtype=jnp.int32)[:, None]
    allowed = (jnp.abs(offset) <= radius) & valid[None, :]
    same = (seg_rows[:, None] == seg_ext[None, :]).astype(jnp.float32)
    scores = scores + bias[:, None, None] * same[None]
    scores = jnp.where(allowed[None], scores, masked_fill)
    gscores = jnp.einsum('thd,ghd->htg', queries, gkeys, preferred_element_type=jnp.float32) * scaling
    top = jnp.maximum(lax.optimization_barrier(jnp.max(scores, axis=-1)), lax.optimization_barrier(jnp.max(gscores, axis=-1)))
    probs = jnp.exp(scores - top[..., None])
    gprobs = jnp.exp(gscores - top[..., None])
    total = lax.optimization_barrier(jnp.sum(probs, axis=-1)) + lax.optimization_barrier(jnp.sum(gprobs, axis=-1))
    mixed = jnp.einsum('hts,shd->thd', probs.astype(jnp.bfloat16), values_ext, preferred_element_type=jnp.float32)
    mixed = mixed + jnp.einsum('htg,ghd->thd', gprobs.astype(jnp.bfloat16), gvalues, preferred_element_type=jnp.float32)
    return (mixed / jnp.transpose(total)[:, :, None]).reshape(rows, -1).astype(jnp.bfloat16)

def partial_global(gqueries, keys_loc, values_loc, seg_rows, table, scaling):
    scores = jnp.einsum('ghd,thd->ght', gqueries, keys_loc, preferred_element_type=jnp.float32) * scaling
    member = (table[:, None] == seg_rows[None, :])[:, None, :]
    scores = jnp.where(member, scores, masked_fill)
    top = lax.optimization_barrier(jnp.max(scores, axis=-1))
    probs = jnp.where(member, jnp.exp(scores - top[..., None]), jnp.float32(0.0))
    total = lax.optimization_barrier(jnp.sum(probs, axis=-1))
    weighted = jnp.einsum('ght,thd->ghd', probs, values_loc.astype(jnp.float32), precision=lax.Precision.HIGHEST)
    return (top, total, weighted)

def self_global(gqueries, gkeys, gvalues, scaling):
    scores = jnp.einsum('ghd,khd->ghk', gqueries, gkeys, preferred_element_type=jnp.float32) * scaling
    top = lax.optimization_barrier(jnp.max(scores, axis=-1))
    probs = jnp.exp(scores - top[..., None])
    total = lax.optimization_barrier(jnp.sum(probs, axis=-1))
    weighted = jnp.einsum('ghk,khd->ghd', probs, gvalues.astype(jnp.float32), precision=lax.Precision.HIGHEST)
    return (top, total, weighted)

def combine_parts(first, second):
    top = jnp.maximum(first[0], second[0])
    factor_a = jnp.exp(first[0] - top)
    factor_b = jnp.exp(second[0] - top)
    total = first[1] * factor_a + second[1] * factor_b
    weighted = first[2] * factor_a[..., None] + second[2] * factor_b[..., None]
    return (top, total, weighted)

def reference(tokens, globals_in, seg_ids, global_table, w_qkv, w_out, gain_local, gain_global, seg_bias):
    head_dim = D // H
    scaling = 1.0 / math.sqrt(head_dim)
    stream = tokens.astype(jnp.float32)
    gstate = globals_in.astype(jnp.float32)
    position = jnp.arange(SEQ + 2 * RADIUS, dtype=jnp.int32) - RADIUS
    valid_all = (position >= 0) & (position < SEQ)
    seg_padded = jnp.pad(seg_ids, (RADIUS, RADIUS), constant_values=-1)
    blocks = SEQ // TOK_DEV
    for layer_no in range(LAYERS):
        normed = layer_norm(stream, gain_local[layer_no])
        gnormed = layer_norm(gstate, gain_global[layer_no])
        proj = jnp.dot(normed, w_qkv[layer_no], preferred_element_type=jnp.float32).astype(jnp.bfloat16)
        gproj = jnp.dot(gnormed, w_qkv[layer_no], preferred_element_type=jnp.float32).astype(jnp.bfloat16)
        queries = proj[:, :D].reshape(SEQ, H, head_dim)
        keys_loc = proj[:, D:2 * D].reshape(SEQ, H, head_dim)
        values_loc = proj[:, 2 * D:].reshape(SEQ, H, head_dim)
        gqueries = gproj[:, :D].reshape(G, H, head_dim)
        gkeys = gproj[:, D:2 * D].reshape(G, H, head_dim)
        gvalues = gproj[:, 2 * D:].reshape(G, H, head_dim)
        keys_pad = jnp.pad(keys_loc, ((RADIUS, RADIUS), (0, 0), (0, 0)))
        values_pad = jnp.pad(values_loc, ((RADIUS, RADIUS), (0, 0), (0, 0)))
        bias = seg_bias[layer_no]

        def local_block(index):
            start = (index * TOK_DEV).astype(jnp.int32)
            span = TOK_DEV + 2 * RADIUS
            return window_attend(lax.dynamic_slice_in_dim(queries, start, TOK_DEV, 0), lax.dynamic_slice_in_dim(keys_pad, start, span, 0), lax.dynamic_slice_in_dim(values_pad, start, span, 0), lax.dynamic_slice_in_dim(seg_ids, start, TOK_DEV, 0), lax.dynamic_slice_in_dim(seg_padded, start, span, 0), lax.dynamic_slice_in_dim(valid_all, start, span, 0), gkeys, gvalues, bias, scaling)
        local_mix = lax.map(local_block, jnp.arange(blocks, dtype=jnp.int32)).reshape(SEQ, D)
        outer = partial_global(gqueries, keys_loc, values_loc, seg_ids, global_table, scaling)
        inner = self_global(gqueries, gkeys, gvalues, scaling)
        merged = combine_parts(outer, inner)
        global_mix = (merged[2] / merged[1][..., None]).reshape(G, D).astype(jnp.bfloat16)
        stream = stream + jnp.dot(local_mix, w_out[layer_no], preferred_element_type=jnp.float32)
        gstate = gstate + jnp.dot(global_mix, w_out[layer_no], preferred_element_type=jnp.float32)
    return (stream.astype(jnp.bfloat16), gstate.astype(jnp.bfloat16))
```

```python
import functools

import jax
import jax.numpy as jnp
from jax import lax
from jax.experimental import pallas as pl
from jax.experimental.pallas import tpu as pltpu
from jax.sharding import PartitionSpec as P

LAYERS = 2
BLK = 128
GROWS = 8
NEG = -1e30
F32 = jnp.float32
BF16 = jnp.bfloat16
NT = (((1,), (1,)), ((), ()))


def norm_rows(values, gain):
    average = jnp.mean(values, axis=-1, keepdims=True)
    centered = values - average
    variance = jnp.mean(centered * centered, axis=-1, keepdims=True)
    return centered * lax.rsqrt(variance + 1e-05) * gain


def three_parts(x):
    hi = x.astype(BF16).astype(F32)
    rest = x - hi
    mid = rest.astype(BF16).astype(F32)
    return hi, mid, (rest - mid).astype(BF16).astype(F32)


def fold(rows):
    half = rows.shape[1] // 2
    return jnp.concatenate([rows[:, :half], rows[:, half:]], axis=0)


def kernel(
    n, owners, heads,
    tok_ref, glob_ref, seg_ref, table_ref, wqkv_hbm, wout_hbm, gl_ref, gg_ref, bias_ref,
    out_ref, gout_ref,
    wqkv, wout, wvt, xa, xh, seg_own, seg_halo,
    qe, qo, ks, vt, kh, vht, e_own, e_halo, e_glob,
    o_a, m_a, l_a, mixt, stream, gstate, gown, rs_src, rs_buf, ag_buf,
    w_sem, seg_send, seg_recv, h_send, h_recv, rs_send, rs_recv, ag_send, ag_recv,
):
    rows, width = tok_ref.shape
    gcount = glob_ref.shape[0]
    head_dim = width // heads
    me = lax.axis_index("seq")
    has_left = me > 0
    has_right = me < n - 1
    left = jnp.maximum(me - 1, 0)
    right = jnp.minimum(me + 1, n - 1)

    barrier = pltpu.get_barrier_semaphore()

    @pl.loop(1, n)
    def _(r):
        pl.semaphore_signal(
            barrier, inc=1, device_id={"seq": lax.rem(me + r, n)},
            device_id_type=pl.DeviceIdType.MESH,
        )

    wcopies = []
    for l in range(LAYERS):
        wcopies.append(pltpu.make_async_copy(wqkv_hbm.at[l], wqkv.at[l], w_sem.at[l]))
    wcopies.append(pltpu.make_async_copy(wout_hbm, wout, w_sem.at[LAYERS]))
    for c in wcopies:
        c.start()

    seg_own[...] = jnp.zeros(seg_own.shape, F32)
    seg_own[0:2, :] = seg_ref[...].astype(F32)

    @pl.when(jnp.logical_not(has_left))
    def _():
        seg_halo[0] = jnp.zeros(seg_halo.shape[1:], F32)
        for l in range(LAYERS):
            xh[l, 0:rows, :] = jnp.zeros((rows, width), BF16)

    @pl.when(jnp.logical_not(has_right))
    def _():
        seg_halo[1] = jnp.zeros(seg_halo.shape[1:], F32)
        for l in range(LAYERS):
            xh[l, rows : 2 * rows, :] = jnp.zeros((rows, width), BF16)

    stream[...] = tok_ref[...].astype(F32)
    xa[0, 0:rows, :] = norm_rows(stream[...], gl_ref[0:1, :]).astype(BF16)
    pl.semaphore_wait(barrier, n - 1)

    def remote(src, dst, ssem, rsem, target):
        return pltpu.make_async_remote_copy(
            src_ref=src, dst_ref=dst, send_sem=ssem, recv_sem=rsem,
            device_id={"seq": target}, device_id_type=pl.DeviceIdType.MESH,
        )

    def halo_to_right(l):
        return remote(
            xa.at[l, pl.ds(0, rows)], xh.at[l, pl.ds(0, rows)], h_send.at[l, 0], h_recv.at[l, 0], right
        )

    def halo_to_left(l):
        return remote(
            xa.at[l, pl.ds(0, rows)], xh.at[l, pl.ds(rows, rows)], h_send.at[l, 1], h_recv.at[l, 1], left
        )

    def seg_to_right():
        return remote(seg_own, seg_halo.at[0], seg_send.at[0], seg_recv.at[0], right)

    def seg_to_left():
        return remote(seg_own, seg_halo.at[1], seg_send.at[1], seg_recv.at[1], left)

    def send_halo(l):
        @pl.when(has_right)
        def _():
            halo_to_right(l).start()

        @pl.when(has_left)
        def _():
            halo_to_left(l).start()

    def wait_halo(l):
        @pl.when(has_left)
        def _():
            halo_to_right(l).wait_recv()

        @pl.when(has_right)
        def _():
            halo_to_left(l).wait_recv()

    send_halo(0)

    @pl.when(has_right)
    def _():
        seg_to_right().start()

    @pl.when(has_left)
    def _():
        seg_to_left().start()

    all_own = n == owners

    def only_owner(body):
        if all_own:
            body()
        else:
            pl.when(me < owners)(body)

    def others(count, body):
        if count == n:
            @pl.loop(1, n)
            def _(r):
                body(lax.rem(me + r, n))
        else:
            @pl.loop(0, count)
            def _(r):
                @pl.when(r != me)
                def _():
                    body(r)

    def rs_copy(l, target, source):
        return remote(
            rs_src.at[l, target], rs_buf.at[l, source], rs_send.at[l, target], rs_recv.at[l, source], target
        )

    def ag_copy(l, target, source):
        return remote(
            ag_buf.at[l, source], ag_buf.at[l, source], ag_send.at[l, target], ag_recv.at[l, source], target
        )

    gstate[...] = glob_ref[...].astype(F32)

    def take_own():
        gown[...] = gstate[pl.ds(me * GROWS, GROWS), :]

    only_owner(take_own)
    xa[0, rows : rows + gcount, :] = norm_rows(gstate[...], gg_ref[0:1, :]).astype(BF16)

    def down(row):
        return jnp.transpose(jnp.broadcast_to(row, (BLK, BLK)))

    for kb in range(2):
        column = down(seg_own[kb : kb + 1, :])
        for rb in range(2):
            row = jnp.broadcast_to(seg_own[rb : rb + 1, :], (BLK, BLK))
            e_own[rb, kb * BLK : (kb + 1) * BLK, :] = jnp.where(column == row, 1.0, 0.0).astype(F32)
        trow = jnp.broadcast_to(table_ref[...].astype(F32), (BLK, BLK))
        e_glob[kb * BLK : (kb + 1) * BLK, :] = jnp.where(column == trow, 0.0, NEG).astype(F32)
    first = jnp.where(me == 0, 0.0, NEG).astype(F32)
    e_glob[2 * BLK : 2 * BLK + gcount, :] = jnp.full((gcount, BLK), 0.0, F32) + first

    lane = lax.broadcasted_iota(jnp.int32, (1, width), 1)
    even = jnp.where(lax.rem(lane // head_dim, 2) == 0, 0.125, 0.0).astype(F32)
    odd = 0.125 - even

    pick = lax.broadcasted_iota(jnp.int32, (BLK, width), 0)
    head_of = lax.broadcasted_iota(jnp.int32, (BLK, width), 1) // head_dim

    def expander(base):
        hit = (pick == base + head_of) | (pick == base + 8 + head_of) | (pick == base + 16 + head_of)
        return jnp.where(hit, 1.0, 0.0).astype(F32).astype(BF16)

    def project(l, lo, count):
        x = xa[l, lo : lo + count, :]
        q = jnp.dot(x, wqkv[l, :, 0:width], preferred_element_type=F32)
        qe[lo : lo + count, :] = (q * even).astype(BF16)
        qo[lo : lo + count, :] = (q * odd).astype(BF16)
        ks[lo : lo + count, :] = jnp.dot(
            x, wqkv[l, :, width : 2 * width], preferred_element_type=F32
        ).astype(BF16)
        vt[:, lo : lo + count] = lax.dot_general(
            wvt[l], x, NT, preferred_element_type=F32
        ).astype(BF16)

    def attend(h, k_ref, v_ref, k0, count, q0, table):
        pair = pl.ds((h // 2) * 2 * head_dim, 2 * head_dim)
        q_ref = qe if h % 2 == 0 else qo
        s = lax.dot_general(
            k_ref[k0 : k0 + count, pair], q_ref[q0 : q0 + BLK, pair], NT, preferred_element_type=F32
        )
        s = table(s)
        top = jnp.max(s, axis=0, keepdims=True)
        p = jnp.exp(s - top)
        total = jnp.sum(p, axis=0, keepdims=True)
        mixed = jnp.dot(
            v_ref[h * head_dim : (h + 1) * head_dim, k0 : k0 + count],
            p.astype(BF16), preferred_element_type=F32,
        )
        return top, total, mixed

    span = rows + gcount

    def global_part(l):
        tops, totals, parts = [], [], []
        for h in range(heads):
            top, total, mixed = attend(h, ks, vt, 0, span, rows, lambda s: s + e_glob[...])
            tops.append(top)
            totals.append(total)
            parts.append(mixed)
        stats = three_parts(jnp.concatenate(tops, axis=0)) + three_parts(jnp.concatenate(totals, axis=0))
        pad = jnp.zeros((BLK - 6 * heads, BLK), F32)
        packed = jnp.transpose(jnp.concatenate(parts + list(stats) + [pad], axis=0))
        half = width // 2
        tail = packed[:, width:]
        upper = jnp.concatenate([packed[:, :half], tail], axis=1)
        lower = jnp.concatenate([packed[:, half:width], tail], axis=1)
        for o in range(owners):
            cut = slice(o * GROWS, (o + 1) * GROWS)
            rs_src[l, o] = jnp.concatenate([upper[cut], lower[cut]], axis=0).astype(BF16)
        others(owners, lambda peer: rs_copy(l, peer, me).start())

    def combine(l):
        rs_buf[l, me] = rs_src[l, me]
        others(n, lambda peer: rs_copy(l, me, peer).wait_recv())
        half = width // 2
        got = rs_buf[l].astype(F32)
        upper = got[:, :GROWS, :]
        lower = got[:, GROWS:, :]
        stats = upper[:, :, half:].reshape(n * GROWS, BLK).astype(BF16)
        top = jnp.dot(stats, expander(0), preferred_element_type=F32).reshape(n, GROWS, width)
        total = jnp.dot(stats, expander(24), preferred_element_type=F32).reshape(n, GROWS, width)
        value = jnp.concatenate([upper[:, :, :half], lower[:, :, :half]], axis=2)
        factor = jnp.exp(top - jnp.max(top, axis=0, keepdims=True))
        mix = jnp.sum(value * factor, axis=0) / jnp.sum(total * factor, axis=0)
        mix = jnp.concatenate([mix, mix], axis=0).astype(BF16)
        new = gown[...] + jnp.dot(mix, wout[l], preferred_element_type=F32)[:GROWS]
        gown[...] = new
        if l + 1 < LAYERS:
            new = norm_rows(new, gg_ref[l + 1 : l + 2, :])
        ag_buf[l, me] = fold(new).astype(BF16)
        others(n, lambda peer: ag_copy(l, peer, me).start())

    def gathered(l):
        others(owners, lambda peer: ag_copy(l, me, peer).wait_recv())
        got = ag_buf[l].astype(F32)
        half = width // 2
        return jnp.concatenate(
            [got[:, :GROWS].reshape(gcount, half), got[:, GROWS:].reshape(gcount, half)], axis=1
        ).astype(BF16)

    for l in range(LAYERS):
        if l == 0:
            for c in wcopies:
                c.wait()
            for w in range(LAYERS):
                wvt[w] = jnp.transpose(wqkv[w, :, 2 * width : 3 * width])
            project(0, 0, span)
        else:
            project(l, 0, rows)
            xa[l, rows:span, :] = gathered(l - 1)
            project(l, rows, gcount)

        global_part(l)

        for rb in range(2):
            for h in range(heads):
                b = bias_ref[l, h]

                def own_table(s):
                    return jnp.concatenate([s[:rows] + e_own[rb] * b, s[rows:]], axis=0)

                top, total, mixed = attend(h, ks, vt, 0, span, rb * BLK, own_table)
                m_a[rb, h : h + 1, :] = top
                l_a[rb, h : h + 1, :] = total
                o_a[rb, h * head_dim : (h + 1) * head_dim, :] = mixed

        wait_halo(l)
        if l == 0:
            @pl.when(has_left)
            def _():
                seg_to_right().wait_recv()

            @pl.when(has_right)
            def _():
                seg_to_left().wait_recv()

            r = lax.broadcasted_iota(jnp.int32, (BLK, BLK), 0)
            c = lax.broadcasted_iota(jnp.int32, (BLK, BLK), 1)
            for t in range(4):
                side, part = t // 2, t % 2
                column = down(seg_halo[side, part : part + 1, :])
                present = has_left if side == 0 else has_right
                absent = jnp.where(present, 0.0, NEG).astype(F32)
                for rb in range(2):
                    if not 0 <= t - rb < 3:
                        continue
                    row = jnp.broadcast_to(seg_own[rb : rb + 1, :], (BLK, BLK))
                    same = jnp.where(column == row, 1.0, 0.0).astype(F32)
                    if side == 0:
                        allowed = r + part * BLK >= c + rb * BLK
                    else:
                        allowed = r + part * BLK <= c + rb * BLK
                    e_halo[rb, (t - rb) * BLK : (t - rb + 1) * BLK, :] = (
                        jnp.where(allowed, same, NEG) + absent
                    )

        x = xh[l]
        kh[...] = jnp.dot(x, wqkv[l, :, width : 2 * width], preferred_element_type=F32).astype(BF16)
        vht[...] = lax.dot_general(wvt[l], x, NT, preferred_element_type=F32).astype(BF16)

        for rb in range(2):
            for h in range(heads):
                b = bias_ref[l, h]
                top_b, total_b, mixed_b = attend(
                    h, kh, vht, rb * BLK, 3 * BLK, rb * BLK, lambda s: s + e_halo[rb] * b
                )
                top_a = m_a[rb, h : h + 1, :]
                top = jnp.maximum(top_a, top_b)
                fa = jnp.exp(top_a - top)
                fb = jnp.exp(top_b - top)
                inv = 1.0 / (l_a[rb, h : h + 1, :] * fa + total_b * fb)
                mixt[h * head_dim : (h + 1) * head_dim, rb * BLK : (rb + 1) * BLK] = (
                    o_a[rb, h * head_dim : (h + 1) * head_dim, :] * (fa * inv) + mixed_b * (fb * inv)
                )
            if rb == 0:
                only_owner(functools.partial(combine, l))

        mix = jnp.transpose(mixt[...]).astype(BF16)
        new = stream[...] + jnp.dot(mix, wout[l], preferred_element_type=F32)
        if l + 1 < LAYERS:
            stream[...] = new
            xa[l + 1, 0:rows, :] = norm_rows(new, gl_ref[l + 1 : l + 2, :]).astype(BF16)
            send_halo(l + 1)
        else:
            out_ref[...] = new.astype(BF16)

    gout_ref[...] = gathered(LAYERS - 1)

    @pl.when(has_right)
    def _():
        seg_to_right().wait_send()
        for l in range(LAYERS):
            halo_to_right(l).wait_send()

    @pl.when(has_left)
    def _():
        seg_to_left().wait_send()
        for l in range(LAYERS):
            halo_to_left(l).wait_send()

    for l in range(LAYERS):
        others(owners, lambda peer: rs_copy(l, peer, me).wait_send())
        only_owner(lambda: others(n, lambda peer: ag_copy(l, peer, me).wait_send()))


def per_device(n, tokens, globals_in, seg_ids, table, w_qkv, w_out, gain_local, gain_global, seg_bias):
    rows, width = tokens.shape
    gcount = globals_in.shape[0]
    heads = seg_bias.shape[1]
    assert rows == 2 * BLK and gcount == BLK and heads == 8
    owners = min(n, gcount // GROWS)
    assert owners * GROWS == gcount
    span = rows + gcount
    vmem = pl.BlockSpec(memory_space=pltpu.VMEM)
    hbm = pl.BlockSpec(memory_space=pl.ANY)
    smem = pl.BlockSpec(memory_space=pltpu.SMEM)
    dma = pltpu.SemaphoreType.DMA
    V = pltpu.VMEM
    half = width // 2
    return pl.pallas_call(
        functools.partial(kernel, n, owners, heads),
        out_shape=(
            jax.ShapeDtypeStruct((rows, width), BF16),
            jax.ShapeDtypeStruct((gcount, width), BF16),
        ),
        in_specs=[vmem, vmem, vmem, vmem, hbm, hbm, vmem, vmem, smem],
        out_specs=(vmem, vmem),
        scratch_shapes=[
            V((LAYERS, width, 3 * width), BF16),
            V((LAYERS, width, width), BF16),
            V((LAYERS, width, width), BF16),
            V((LAYERS, span, width), BF16),
            V((LAYERS, 2 * rows, width), BF16),
            V((8, BLK), F32),
            V((2, 8, BLK), F32),
            V((span, width), BF16),
            V((span, width), BF16),
            V((span, width), BF16),
            V((width, span), BF16),
            V((2 * rows, width), BF16),
            V((width, 2 * rows), BF16),
            V((2, rows, BLK), F32),
            V((2, 3 * BLK, BLK), F32),
            V((span, BLK), F32),
            V((2, width, BLK), F32),
            V((2, heads, BLK), F32),
            V((2, heads, BLK), F32),
            V((width, rows), F32),
            V((rows, width), F32),
            V((gcount, width), F32),
            V((GROWS, width), F32),
            V((LAYERS, owners, 2 * GROWS, half + BLK), BF16),
            V((LAYERS, n, 2 * GROWS, half + BLK), BF16),
            V((LAYERS, owners, 2 * GROWS, half), BF16),
            dma((LAYERS + 1,)),
            dma((2,)),
            dma((2,)),
            dma((LAYERS, 2)),
            dma((LAYERS, 2)),
            dma((LAYERS, owners)),
            dma((LAYERS, n)),
            dma((LAYERS, n)),
            dma((LAYERS, owners)),
        ],
        compiler_params=pltpu.CompilerParams(
            collective_id=0, has_side_effects=True, vmem_limit_bytes=40 * 1024 * 1024
        ),
        name="encoder",
    )(
        tokens, globals_in, seg_ids.reshape(2, BLK), table.reshape(1, BLK),
        w_qkv, w_out, gain_local, gain_global, seg_bias,
    )


def solution(mesh):
    return jax.shard_map(
        functools.partial(per_device, mesh.shape["seq"]),
        mesh=mesh,
        in_specs=(
            P(("dp", "seq"), None),
            P("dp", None),
            P(("dp", "seq")),
            P("dp"),
            P(),
            P(),
            P(),
            P(),
            P(),
        ),
        out_specs=(P(("dp", "seq"), None), P("dp", None)),
        check_vma=False,
    )
```

```python
import functools

import jax
import jax.numpy as jnp
from jax import lax
from jax.experimental import pallas as pl
from jax.experimental.pallas import tpu as pltpu
from jax.sharding import PartitionSpec as P

LAYERS = 2
BLK = 128
GROWS = 8
IDS = 64
ONES = 16
NEG = -1e30
F32 = jnp.float32
BF16 = jnp.bfloat16
NT = (((1,), (1,)), ((), ()))


def norm_rows(values, gain):
    average = jnp.mean(values, axis=-1, keepdims=True)
    centered = values - average
    variance = jnp.mean(centered * centered, axis=-1, keepdims=True)
    return centered * lax.rsqrt(variance + 1e-05) * gain


def three_parts(x):
    hi = x.astype(BF16).astype(F32)
    rest = x - hi
    mid = rest.astype(BF16).astype(F32)
    return hi, mid, (rest - mid).astype(BF16).astype(F32)


def fold(rows):
    half = rows.shape[1] // 2
    return jnp.concatenate([rows[:, :half], rows[:, half:]], axis=0)


def kernel(
    n, owners, heads,
    tok_hbm, glob_hbm, seg_hbm, table_hbm, wqkv_hbm, wout_hbm, gl_hbm, gg_hbm, bias_hbm,
    out_ref, gout_ref,
    tok_ref, glob_ref, seg_ref, table_ref, wqkv, wout, gl_ref, gg_ref, bias_ref,
    wvt, xa, xh, seg_own, seg_halo,
    qs, k_own, v_own, k_far, v_far, tri,
    o_a, m_a, l_a, mixt, stream, gall, gown, rs_src, rs_buf, ag_buf,
    in_sem, seg_send, seg_recv, h_send, h_recv, rs_send, rs_recv, ag_send, ag_recv,
):
    rows, width = tok_ref.shape
    gcount = glob_ref.shape[0]
    head_dim = width // heads
    me = lax.axis_index("seq")
    has_left = me > 0
    has_right = me < n - 1
    left = jnp.maximum(me - 1, 0)
    right = jnp.minimum(me + 1, n - 1)

    barrier = pltpu.get_barrier_semaphore()

    @pl.loop(1, n)
    def _(r):
        pl.semaphore_signal(
            barrier, inc=1, device_id={"seq": lax.rem(me + r, n)},
            device_id_type=pl.DeviceIdType.MESH,
        )

    def load(i, src, dst):
        copy = pltpu.make_async_copy(src, dst, in_sem.at[i])
        copy.start()
        return copy

    tok_in = load(0, tok_hbm, tok_ref)
    gl_in = load(1, gl_hbm, gl_ref)
    seg_in = load(2, seg_hbm, seg_ref)
    w_in = [load(3, wqkv_hbm.at[0], wqkv.at[0])]
    small_in = [
        load(4, glob_hbm, glob_ref),
        load(5, table_hbm, table_ref),
        load(6, gg_hbm, gg_ref),
        load(7, bias_hbm, bias_ref),
    ]
    wout_in = load(8, wout_hbm, wout)
    w_in += [load(8 + l, wqkv_hbm.at[l], wqkv.at[l]) for l in range(1, LAYERS)]

    pairs = heads // 2
    wide = 2 * BLK
    seg_in.wait()
    seg_own[...] = jnp.zeros(seg_own.shape, F32)
    seg_own[0:2, :] = seg_ref[...].astype(F32)

    @pl.when(jnp.logical_not(has_left))
    def _():
        seg_halo[0] = jnp.zeros(seg_halo.shape[1:], F32)
        for l in range(LAYERS):
            xh[l, 0:rows, :] = jnp.zeros((rows, width), BF16)

    @pl.when(jnp.logical_not(has_right))
    def _():
        seg_halo[1] = jnp.zeros(seg_halo.shape[1:], F32)
        for l in range(LAYERS):
            xh[l, rows : 2 * rows, :] = jnp.zeros((rows, width), BF16)

    tok_in.wait()
    gl_in.wait()
    stream[...] = tok_ref[...].astype(F32)
    xa[0, 0:rows, :] = norm_rows(stream[...], gl_ref[0:1, :]).astype(BF16)
    pl.semaphore_wait(barrier, n - 1)

    def remote(src, dst, ssem, rsem, target):
        return pltpu.make_async_remote_copy(
            src_ref=src, dst_ref=dst, send_sem=ssem, recv_sem=rsem,
            device_id={"seq": target}, device_id_type=pl.DeviceIdType.MESH,
        )

    def halo_to_right(l):
        return remote(
            xa.at[l, pl.ds(0, rows)], xh.at[l, pl.ds(0, rows)], h_send.at[l, 0], h_recv.at[l, 0], right
        )

    def halo_to_left(l):
        return remote(
            xa.at[l, pl.ds(0, rows)], xh.at[l, pl.ds(rows, rows)], h_send.at[l, 1], h_recv.at[l, 1], left
        )

    def seg_to_right():
        return remote(seg_own, seg_halo.at[0], seg_send.at[0], seg_recv.at[0], right)

    def seg_to_left():
        return remote(seg_own, seg_halo.at[1], seg_send.at[1], seg_recv.at[1], left)

    def send_halo(l):
        @pl.when(has_right)
        def _():
            halo_to_right(l).start()

        @pl.when(has_left)
        def _():
            halo_to_left(l).start()

    def wait_halo(l):
        @pl.when(has_left)
        def _():
            halo_to_right(l).wait_recv()

        @pl.when(has_right)
        def _():
            halo_to_left(l).wait_recv()

    send_halo(0)

    @pl.when(has_right)
    def _():
        seg_to_right().start()

    @pl.when(has_left)
    def _():
        seg_to_left().start()

    all_own = n == owners

    def only_owner(body):
        if all_own:
            body()
        else:
            pl.when(me < owners)(body)

    def others(count, body):
        if count == n:
            @pl.loop(1, n)
            def _(r):
                body(lax.rem(me + r, n))
        else:
            @pl.loop(0, count)
            def _(r):
                @pl.when(r != me)
                def _():
                    body(r)

    def rs_copy(l, target, source):
        return remote(
            rs_src.at[l, target], rs_buf.at[l, source], rs_send.at[l, target], rs_recv.at[l, source], target
        )

    def ag_copy(l, target, source):
        return remote(
            ag_buf.at[l, source], ag_buf.at[l, source], ag_send.at[l, target], ag_recv.at[l, source], target
        )

    for copy in small_in:
        copy.wait()

    xa[0, rows : rows + gcount, :] = norm_rows(glob_ref[...].astype(F32), gg_ref[0:1, :]).astype(BF16)
    gall[...] = glob_ref[...].astype(F32)

    def take_own():
        gown[...] = gall[pl.ds(me * GROWS, GROWS), :]

    only_owner(take_own)

    lane = lax.broadcasted_iota(jnp.int32, (BLK, BLK), 1)
    lane_id = lax.rem(lane, IDS)
    lane_idf = lane_id.astype(F32)
    low = lane < IDS

    def down(row):
        return jnp.transpose(jnp.broadcast_to(row, (BLK, BLK)))

    def marks(row):
        return jnp.where(down(row) == lane_idf, 1.0, 0.0).astype(F32)

    def put_marks(ref, at, value):
        for p in range(pairs):
            ref[at : at + BLK, p * wide + BLK : (p + 1) * wide] = value.astype(BF16)

    outside = jnp.where(lane == 0, NEG, 0.0).astype(F32)
    for rb in range(2):
        own = marks(seg_own[rb : rb + 1, :])
        put_marks(k_own, rb * BLK, own)
        for l in range(LAYERS):
            for h in range(heads):
                b = jnp.broadcast_to(bias_ref[l : l + 1, h : h + 1], (BLK, BLK))
                b_hi = b.astype(BF16).astype(F32)
                qs[l, h // 2, rb, (h % 2) * BLK : (h % 2 + 1) * BLK, BLK:] = (
                    own * jnp.where(low, b_hi, b - b_hi) + outside
                ).astype(BF16)
    hidden = jnp.where(me == 0, 0.0, 1.0).astype(F32)
    g_marks = jnp.where(lane == IDS, 1.0, 0.0).astype(F32) * hidden
    put_marks(k_own, rows, g_marks)
    put_marks(k_far, rows, g_marks)
    member = marks(table_ref[...].astype(F32))
    g_side = jnp.where(low & (lane > 0), (1.0 - member) * NEG, 0.0) + jnp.where(lane == IDS, NEG, 0.0)
    for l in range(LAYERS):
        for h in range(heads):
            qs[l, h // 2, 2, (h % 2) * BLK : (h % 2 + 1) * BLK, BLK:] = g_side.astype(BF16)

    tr = lax.broadcasted_iota(jnp.int32, (BLK, wide), 0)
    tc = lax.rem(lax.broadcasted_iota(jnp.int32, (BLK, wide), 1), BLK)
    tri[0] = jnp.where(tr >= tc, 0.0, NEG).astype(F32)
    tri[1] = jnp.where(tr <= tc, 0.0, NEG).astype(F32)
    v_own[:, BLK:, :] = jnp.ones((pairs, ONES, rows + gcount), BF16)
    v_far[:, BLK:, :] = jnp.ones((pairs, ONES, 2 * rows + gcount), BF16)

    head_lane = lax.broadcasted_iota(jnp.int32, (1, BLK), 1)
    even = jnp.where(head_lane < head_dim, 0.125, 0.0).astype(F32)
    odd = 0.125 - even

    pick = lax.broadcasted_iota(jnp.int32, (BLK, width), 0)
    head_of = lax.broadcasted_iota(jnp.int32, (BLK, width), 1) // head_dim

    def expander(base):
        hit = (pick == base + head_of) | (pick == base + 8 + head_of) | (pick == base + 16 + head_of)
        return jnp.where(hit, 1.0, 0.0).astype(F32).astype(BF16)

    def put_keys(l, x, *places):
        count = x.shape[0]
        k = jnp.dot(x, wqkv[l, :, width : 2 * width], preferred_element_type=F32).astype(BF16)
        v = lax.dot_general(wvt[l], x, NT, preferred_element_type=F32).astype(BF16)
        for k_ref, v_ref, at in places:
            for p in range(pairs):
                k_ref[at : at + count, p * wide : p * wide + BLK] = k[:, p * BLK : (p + 1) * BLK]
                v_ref[p, 0:BLK, at : at + count] = v[p * BLK : (p + 1) * BLK]

    def put_queries(l, x, first):
        q = jnp.dot(x, wqkv[l, :, 0:width], preferred_element_type=F32)
        for b in range(x.shape[0] // BLK):
            for p in range(pairs):
                part = q[b * BLK : (b + 1) * BLK, p * BLK : (p + 1) * BLK]
                qs[l, p, first + b, 0:BLK, 0:BLK] = (part * even).astype(BF16)
                qs[l, p, first + b, BLK:, 0:BLK] = (part * odd).astype(BF16)

    def project_local(l):
        x = xa[l, 0:rows, :]
        put_queries(l, x, 0)
        put_keys(l, x, (k_own, v_own, 0))

    def project_global(l):
        x = xa[l, rows : rows + gcount, :]
        put_queries(l, x, 2)
        put_keys(l, x, (k_own, v_own, rows), (k_far, v_far, rows))

    def attend(l, p, rb, k_ref, v_ref, k0, count, masked=False):
        s = lax.dot_general(
            k_ref[k0 : k0 + count, p * wide : (p + 1) * wide], qs[l, p, rb], NT,
            preferred_element_type=F32,
        )
        if masked:
            s = jnp.concatenate(
                [s[:BLK] + tri[0], s[BLK : count - BLK], s[count - BLK :] + tri[1]], axis=0
            )
        top = jnp.max(s, axis=0, keepdims=True)
        probs = jnp.exp(s - top).astype(BF16)
        mixed = jnp.dot(v_ref[p, :, k0 : k0 + count], probs, preferred_element_type=F32)
        value = jnp.concatenate([mixed[:head_dim, :BLK], mixed[head_dim:BLK, BLK:]], axis=1)
        return top, mixed[BLK : BLK + 1], value

    span = rows + gcount

    def global_part(l):
        tops, totals, parts = [], [], []
        for p in range(pairs):
            top, total, value = attend(l, p, 2, k_own, v_own, 0, span)
            for lanes in (slice(0, BLK), slice(BLK, wide)):
                tops.append(top[:, lanes])
                totals.append(total[:, lanes])
                parts.append(value[:, lanes])
        stats = three_parts(jnp.concatenate(tops, axis=0)) + three_parts(jnp.concatenate(totals, axis=0))
        pad = jnp.zeros((BLK - 6 * heads, BLK), F32)
        packed = jnp.transpose(jnp.concatenate(parts + list(stats) + [pad], axis=0))
        half = width // 2
        tail = packed[:, width:]
        upper = jnp.concatenate([packed[:, :half], tail], axis=1)
        lower = jnp.concatenate([packed[:, half:width], tail], axis=1)
        for o in range(owners):
            cut = slice(o * GROWS, (o + 1) * GROWS)
            rs_src[l, o] = jnp.concatenate([upper[cut], lower[cut]], axis=0).astype(BF16)
        others(owners, lambda peer: rs_copy(l, peer, me).start())

    def combine(l):
        rs_buf[l, me] = rs_src[l, me]
        others(n, lambda peer: rs_copy(l, me, peer).wait_recv())
        half = width // 2
        got = rs_buf[l].astype(F32)
        upper = got[:, :GROWS, :]
        lower = got[:, GROWS:, :]
        stats = upper[:, :, half:].reshape(n * GROWS, BLK).astype(BF16)
        top = jnp.dot(stats, expander(0), preferred_element_type=F32).reshape(n, GROWS, width)
        total = jnp.dot(stats, expander(24), preferred_element_type=F32).reshape(n, GROWS, width)
        value = jnp.concatenate([upper[:, :, :half], lower[:, :, :half]], axis=2)
        factor = jnp.exp(top - jnp.max(top, axis=0, keepdims=True))
        mix = jnp.sum(value * factor, axis=0) / jnp.sum(total * factor, axis=0)
        mix = jnp.concatenate([mix, mix], axis=0).astype(BF16)
        new = gown[...] + jnp.dot(mix, wout[l], preferred_element_type=F32)[:GROWS]
        gown[...] = new
        if l + 1 < LAYERS:
            new = norm_rows(new, gg_ref[l + 1 : l + 2, :])
        ag_buf[l, me] = fold(new).astype(BF16)
        others(n, lambda peer: ag_copy(l, peer, me).start())

    def gathered(l):
        others(owners, lambda peer: ag_copy(l, me, peer).wait_recv())
        got = ag_buf[l].astype(F32)
        half = width // 2
        return jnp.concatenate(
            [got[:, :GROWS].reshape(gcount, half), got[:, GROWS:].reshape(gcount, half)], axis=1
        ).astype(BF16)

    def near_part(l):
        for rb in range(2):
            for p in range(pairs):
                top, total, value = attend(l, p, rb, k_own, v_own, 0, rows)
                m_a[rb, p] = top
                l_a[rb, p] = total
                o_a[rb, p] = value

    def turn(l):
        w_in[l].wait()
        wvt[l] = jnp.transpose(wqkv[l, :, 2 * width : 3 * width])

    for l in range(LAYERS):
        if l == 0:
            turn(0)
            project_global(0)
            project_local(0)
            global_part(0)
            near_part(0)
            wout_in.wait()
            for w in range(1, LAYERS):
                turn(w)
        else:
            project_local(l)
            near_part(l)
            xa[l, rows:span, :] = gathered(l - 1)
            project_global(l)
            global_part(l)

        wait_halo(l)
        if l == 0:
            @pl.when(has_left)
            def _():
                seg_to_right().wait_recv()

            @pl.when(has_right)
            def _():
                seg_to_left().wait_recv()

            for side in range(2):
                for part in range(2):
                    put_marks(
                        k_far, side * span + part * BLK, marks(seg_halo[side, part : part + 1, :])
                    )

        put_keys(l, xh[l, 0:rows, :], (k_far, v_far, 0))
        put_keys(l, xh[l, rows : 2 * rows, :], (k_far, v_far, span))
        only_owner(functools.partial(combine, l))

        for rb in range(2):
            for p in range(pairs):
                top_b, total_b, value_b = attend(
                    l, p, rb, k_far, v_far, rb * BLK, 4 * BLK, masked=True
                )
                top_a = m_a[rb, p]
                top = jnp.maximum(top_a, top_b)
                fa = jnp.exp(top_a - top)
                fb = jnp.exp(top_b - top)
                inv = 1.0 / (l_a[rb, p] * fa + total_b * fb)
                value = o_a[rb, p] * (fa * inv) + value_b * (fb * inv)
                lanes = slice(rb * BLK, (rb + 1) * BLK)
                mixt[p * BLK : p * BLK + head_dim, lanes] = value[:, :BLK]
                mixt[p * BLK + head_dim : (p + 1) * BLK, lanes] = value[:, BLK:]

        mix = jnp.transpose(mixt[...]).astype(BF16)
        new = stream[...] + jnp.dot(mix, wout[l], preferred_element_type=F32)
        if l + 1 < LAYERS:
            stream[...] = new
            xa[l + 1, 0:rows, :] = norm_rows(new, gl_ref[l + 1 : l + 2, :]).astype(BF16)
            send_halo(l + 1)
        else:
            out_ref[...] = new.astype(BF16)

    gout_ref[...] = gathered(LAYERS - 1)

    @pl.when(has_right)
    def _():
        seg_to_right().wait_send()
        for l in range(LAYERS):
            halo_to_right(l).wait_send()

    @pl.when(has_left)
    def _():
        seg_to_left().wait_send()
        for l in range(LAYERS):
            halo_to_left(l).wait_send()

    for l in range(LAYERS):
        others(owners, lambda peer: rs_copy(l, peer, me).wait_send())
        only_owner(lambda: others(n, lambda peer: ag_copy(l, peer, me).wait_send()))


def per_device(n, tokens, globals_in, seg_ids, table, w_qkv, w_out, gain_local, gain_global, seg_bias):
    rows, width = tokens.shape
    gcount = globals_in.shape[0]
    heads = seg_bias.shape[1]
    assert rows == 2 * BLK and gcount == BLK and heads == 8
    owners = min(n, gcount // GROWS)
    assert owners * GROWS == gcount
    span = rows + gcount
    vmem = pl.BlockSpec(memory_space=pltpu.VMEM)
    hbm = pl.BlockSpec(memory_space=pltpu.HBM)
    dma = pltpu.SemaphoreType.DMA
    V = pltpu.VMEM
    half = width // 2
    pairs, wide, head_dim = heads // 2, 2 * BLK, width // heads
    assert 2 * head_dim == BLK
    return pl.pallas_call(
        functools.partial(kernel, n, owners, heads),
        out_shape=(
            jax.ShapeDtypeStruct((rows, width), BF16),
            jax.ShapeDtypeStruct((gcount, width), BF16),
        ),
        in_specs=[hbm] * 9,
        out_specs=(vmem, vmem),
        scratch_shapes=[
            V((rows, width), BF16),
            V((gcount, width), BF16),
            V((2, BLK), jnp.int32),
            V((1, BLK), jnp.int32),
            V((LAYERS, width, 3 * width), BF16),
            V((LAYERS, width, width), BF16),
            V((LAYERS, width), F32),
            V((LAYERS, width), F32),
            V((LAYERS, heads), F32),
            V((LAYERS, width, width), BF16),
            V((LAYERS, span, width), BF16),
            V((LAYERS, 2 * rows, width), BF16),
            V((8, BLK), F32),
            V((2, 8, BLK), F32),
            V((LAYERS, pairs, 3, wide, wide), BF16),
            V((span, pairs * wide), BF16),
            V((pairs, BLK + ONES, span), BF16),
            V((2 * rows + gcount, pairs * wide), BF16),
            V((pairs, BLK + ONES, 2 * rows + gcount), BF16),
            V((2, BLK, wide), F32),
            V((2, pairs, head_dim, wide), F32),
            V((2, pairs, 1, wide), F32),
            V((2, pairs, 1, wide), F32),
            V((width, rows), F32),
            V((rows, width), F32),
            V((gcount, width), F32),
            V((GROWS, width), F32),
            V((LAYERS, owners, 2 * GROWS, half + BLK), BF16),
            V((LAYERS, n, 2 * GROWS, half + BLK), BF16),
            V((LAYERS, owners, 2 * GROWS, half), BF16),
            dma((8 + LAYERS,)),
            dma((2,)),
            dma((2,)),
            dma((LAYERS, 2)),
            dma((LAYERS, 2)),
            dma((LAYERS, owners)),
            dma((LAYERS, n)),
            dma((LAYERS, n)),
            dma((LAYERS, owners)),
        ],
        compiler_params=pltpu.CompilerParams(
            collective_id=0, has_side_effects=True, vmem_limit_bytes=40 * 1024 * 1024
        ),
        name="encoder",
    )(
        tokens, globals_in, seg_ids.reshape(2, BLK), table.reshape(1, BLK),
        w_qkv, w_out, gain_local, gain_global, seg_bias,
    )


def solution(mesh):
    return jax.shard_map(
        functools.partial(per_device, mesh.shape["seq"]),
        mesh=mesh,
        in_specs=(
            P(("dp", "seq"), None),
            P("dp", None),
            P(("dp", "seq")),
            P("dp"),
            P(),
            P(),
            P(),
            P(),
            P(),
        ),
        out_specs=(P(("dp", "seq"), None), P("dp", None)),
        check_vma=False,
    )
```

```python
import functools

import jax
import jax.numpy as jnp
from jax import lax
from jax.experimental import pallas as pl
from jax.experimental.pallas import tpu as pltpu
from jax.sharding import PartitionSpec as P

LAYERS = 2
BLK = 128
GROWS = 8
IDS = 64
ONES = 16
VMEM_BYTES = 62 * 1024 * 1024
NEG = -1e30
F32 = jnp.float32
BF16 = jnp.bfloat16


def norm_rows(values, gain):
    average = jnp.mean(values, axis=-1, keepdims=True)
    centered = values - average
    variance = jnp.mean(centered * centered, axis=-1, keepdims=True)
    return centered * lax.rsqrt(variance + 1e-05) * gain


def three_parts(x):
    hi = x.astype(BF16).astype(F32)
    rest = x - hi
    mid = rest.astype(BF16).astype(F32)
    return hi, mid, (rest - mid).astype(BF16).astype(F32)


def fold(rows):
    half = rows.shape[1] // 2
    return jnp.concatenate([rows[:, :half], rows[:, half:]], axis=0)


def kernel(
    n, owners, heads,
    tok_hbm, glob_hbm, seg_hbm, table_hbm, wqkv_hbm, wout_hbm, gl_hbm, gg_hbm, bias_hbm,
    out_ref, gout_ref,
    tok_ref, glob_ref, seg_ref, table_ref, wqkv, wout, gl_ref, gg_ref, bias_ref,
    xa, xh, seg_own, seg_halo,
    qs, k_own, v_own, k_far, v_far, tri, spread,
    o_a, m_a, l_a, mixt, stream, gall, gown, rs_src, rs_buf, ag_buf,
    in_sem, seg_send, seg_recv, h_send, h_recv, rs_send, rs_recv, ag_send, ag_recv,
):
    rows, width = tok_ref.shape
    gcount = glob_ref.shape[0]
    head_dim = width // heads
    me = lax.axis_index("seq")
    has_left = me > 0
    has_right = me < n - 1
    left = jnp.maximum(me - 1, 0)
    right = jnp.minimum(me + 1, n - 1)

    barrier = pltpu.get_barrier_semaphore()

    @pl.loop(1, n)
    def _(r):
        pl.semaphore_signal(
            barrier, inc=1, device_id={"seq": lax.rem(me + r, n)},
            device_id_type=pl.DeviceIdType.MESH,
        )

    def load(i, src, dst):
        copy = pltpu.make_async_copy(src, dst, in_sem.at[i])
        copy.start()
        return copy

    tok_in = load(0, tok_hbm, tok_ref)
    gl_in = load(1, gl_hbm, gl_ref)
    seg_in = load(2, seg_hbm, seg_ref)
    w_in = [load(3, wqkv_hbm.at[0], wqkv.at[0])]
    small_in = [
        load(4, glob_hbm, glob_ref),
        load(5, table_hbm, table_ref),
        load(6, gg_hbm, gg_ref),
        load(7, bias_hbm, bias_ref),
    ]
    wout_in = load(8, wout_hbm, wout)
    w_in += [load(8 + l, wqkv_hbm.at[l], wqkv.at[l]) for l in range(1, LAYERS)]

    pairs = heads // 2
    wide = 2 * BLK
    seg_in.wait()
    seg_own[...] = jnp.zeros(seg_own.shape, F32)
    seg_own[0:2, :] = seg_ref[...].astype(F32)

    @pl.when(jnp.logical_not(has_left))
    def _():
        seg_halo[0] = jnp.zeros(seg_halo.shape[1:], F32)
        for l in range(LAYERS):
            xh[l, 0:rows, :] = jnp.zeros((rows, width), BF16)

    @pl.when(jnp.logical_not(has_right))
    def _():
        seg_halo[1] = jnp.zeros(seg_halo.shape[1:], F32)
        for l in range(LAYERS):
            xh[l, rows : 2 * rows, :] = jnp.zeros((rows, width), BF16)

    tok_in.wait()
    gl_in.wait()
    stream[...] = tok_ref[...].astype(F32)
    xa[0, 0:rows, :] = norm_rows(stream[...], gl_ref[0:1, :]).astype(BF16)
    pl.semaphore_wait(barrier, n - 1)

    def remote(src, dst, ssem, rsem, target):
        return pltpu.make_async_remote_copy(
            src_ref=src, dst_ref=dst, send_sem=ssem, recv_sem=rsem,
            device_id={"seq": target}, device_id_type=pl.DeviceIdType.MESH,
        )

    def halo_to_right(l):
        return remote(
            xa.at[l, pl.ds(0, rows)], xh.at[l, pl.ds(0, rows)], h_send.at[l, 0], h_recv.at[l, 0], right
        )

    def halo_to_left(l):
        return remote(
            xa.at[l, pl.ds(0, rows)], xh.at[l, pl.ds(rows, rows)], h_send.at[l, 1], h_recv.at[l, 1], left
        )

    def seg_to_right():
        return remote(seg_own, seg_halo.at[0], seg_send.at[0], seg_recv.at[0], right)

    def seg_to_left():
        return remote(seg_own, seg_halo.at[1], seg_send.at[1], seg_recv.at[1], left)

    def send_halo(l):
        @pl.when(has_right)
        def _():
            halo_to_right(l).start()

        @pl.when(has_left)
        def _():
            halo_to_left(l).start()

    def wait_halo(l):
        @pl.when(has_left)
        def _():
            halo_to_right(l).wait_recv()

        @pl.when(has_right)
        def _():
            halo_to_left(l).wait_recv()

    send_halo(0)

    @pl.when(has_right)
    def _():
        seg_to_right().start()

    @pl.when(has_left)
    def _():
        seg_to_left().start()

    all_own = n == owners

    def only_owner(body):
        if all_own:
            body()
        else:
            pl.when(me < owners)(body)

    def others(count, body):
        if count == n:
            @pl.loop(1, n)
            def _(r):
                body(lax.rem(me + r, n))
        else:
            @pl.loop(0, count)
            def _(r):
                @pl.when(r != me)
                def _():
                    body(r)

    def rs_copy(l, target, source):
        return remote(
            rs_src.at[l, target], rs_buf.at[l, source], rs_send.at[l, target], rs_recv.at[l, source], target
        )

    def ag_copy(l, target, source):
        return remote(
            ag_buf.at[l, source], ag_buf.at[l, source], ag_send.at[l, target], ag_recv.at[l, source], target
        )

    for copy in small_in:
        copy.wait()

    xa[0, rows : rows + gcount, :] = norm_rows(glob_ref[...].astype(F32), gg_ref[0:1, :]).astype(BF16)
    gall[...] = glob_ref[...].astype(F32)

    def take_own():
        gown[...] = gall[pl.ds(me * GROWS, GROWS), :]

    only_owner(take_own)

    lane = lax.broadcasted_iota(jnp.int32, (BLK, BLK), 1)
    lane_idf = (lane & (IDS - 1)).astype(F32)
    deep = lax.broadcasted_iota(jnp.int32, (BLK, BLK), 0)
    deep_idf = (deep & (IDS - 1)).astype(F32)
    low = deep < IDS

    def down(row):
        return jnp.transpose(jnp.broadcast_to(row, (BLK, BLK)))

    def marks(row):
        return jnp.where(down(row) == lane_idf, 1.0, 0.0).astype(F32)

    def put_marks(ref, at, value):
        for p in range(pairs):
            ref[at : at + BLK, p * wide + BLK : (p + 1) * wide] = value.astype(BF16)

    for l in range(LAYERS):
        for p in range(pairs):
            for b in range(3):
                qs[l, p, b, 0:BLK, :] = jnp.zeros((BLK, wide), BF16)

    outside = jnp.where(deep == 0, NEG, 0.0).astype(F32)
    for rb in range(2):
        row = seg_own[rb : rb + 1, :]
        put_marks(k_own, rb * BLK, marks(row))
        own = jnp.where(jnp.broadcast_to(row, (BLK, BLK)) == deep_idf, 1.0, 0.0).astype(F32)
        for l in range(LAYERS):
            for h in range(heads):
                b = jnp.broadcast_to(bias_ref[l : l + 1, h : h + 1], (BLK, BLK))
                b_hi = b.astype(BF16).astype(F32)
                qs[l, h // 2, rb, BLK:, (h % 2) * BLK : (h % 2 + 1) * BLK] = (
                    own * jnp.where(low, b_hi, b - b_hi) + outside
                ).astype(BF16)
    hidden = jnp.where(me == 0, 0.0, 1.0).astype(F32)
    g_marks = jnp.where(lane == IDS, 1.0, 0.0).astype(F32) * hidden
    put_marks(k_own, rows, g_marks)
    put_marks(k_far, rows, g_marks)
    member = jnp.broadcast_to(table_ref[...].astype(F32), (BLK, BLK)) == deep_idf
    g_side = jnp.where((low & (deep > 0) & jnp.logical_not(member)) | (deep == IDS), NEG, 0.0)
    g_side = g_side.astype(F32).astype(BF16)
    for l in range(LAYERS):
        for p in range(pairs):
            qs[l, p, 2, BLK:, 0:BLK] = g_side
            qs[l, p, 2, BLK:, BLK:] = g_side

    tr = lax.broadcasted_iota(jnp.int32, (BLK, wide), 0)
    tc = lax.broadcasted_iota(jnp.int32, (BLK, wide), 1) & (BLK - 1)
    tri[0] = jnp.where(tr >= tc, 0.0, NEG).astype(F32)
    tri[1] = jnp.where(tr <= tc, 0.0, NEG).astype(F32)
    v_own[:, BLK:, :] = jnp.ones((pairs, ONES, rows + gcount), BF16)
    v_far[:, BLK:, :] = jnp.ones((pairs, ONES, 2 * rows + gcount), BF16)

    pick = lax.broadcasted_iota(jnp.int32, (BLK, width), 0)
    start = lax.broadcasted_iota(jnp.int32, (BLK, width), 1) & (head_dim - 1)
    head_of = (lax.broadcasted_iota(jnp.int32, (BLK, width), 1) - start).astype(F32) * (1.0 / head_dim)
    pick_head = (pick & 7).astype(F32)
    for i in range(2):
        hit = (pick_head == head_of) & (pick >= 24 * i) & (pick < 24 * (i + 1))
        spread[i] = jnp.where(hit, 1.0, 0.0).astype(F32).astype(BF16)

    def put_keys(l, x, *places):
        count = x.shape[0]
        k = jnp.dot(x, wqkv[l, :, width : 2 * width], preferred_element_type=F32).astype(BF16)
        v = jnp.dot(x, wqkv[l, :, 2 * width : 3 * width], preferred_element_type=F32).astype(BF16)
        v = jnp.transpose(v)
        for k_ref, v_ref, at in places:
            for p in range(pairs):
                k_ref[at : at + count, p * wide : p * wide + BLK] = k[:, p * BLK : (p + 1) * BLK]
                v_ref[p, 0:BLK, at : at + count] = v[p * BLK : (p + 1) * BLK]

    def put_queries(l, x, first):
        q = jnp.dot(x, wqkv[l, :, 0:width], preferred_element_type=F32)
        q = jnp.transpose((q * 0.125).astype(BF16))
        for b in range(x.shape[0] // BLK):
            for p in range(pairs):
                lanes = slice(b * BLK, (b + 1) * BLK)
                at = p * BLK
                qs[l, p, first + b, 0:head_dim, 0:BLK] = q[at : at + head_dim, lanes]
                qs[l, p, first + b, head_dim:BLK, BLK:] = q[at + head_dim : at + BLK, lanes]

    def project_local(l):
        x = xa[l, 0:rows, :]
        put_queries(l, x, 0)
        put_keys(l, x, (k_own, v_own, 0))

    def project_global(l):
        x = xa[l, rows : rows + gcount, :]
        put_queries(l, x, 2)
        put_keys(l, x, (k_own, v_own, rows), (k_far, v_far, rows))

    def attend(l, p, rb, k_ref, v_ref, k0, count, masked=False):
        s = jnp.dot(
            k_ref[k0 : k0 + count, p * wide : (p + 1) * wide], qs[l, p, rb],
            preferred_element_type=F32,
        )
        if masked:
            s = jnp.concatenate(
                [s[:BLK] + tri[0], s[BLK : count - BLK], s[count - BLK :] + tri[1]], axis=0
            )
        top = jnp.max(s, axis=0, keepdims=True)
        probs = jnp.exp(s - top).astype(BF16)
        mixed = jnp.dot(v_ref[p, :, k0 : k0 + count], probs, preferred_element_type=F32)
        value = jnp.concatenate([mixed[:head_dim, :BLK], mixed[head_dim:BLK, BLK:]], axis=1)
        return top, mixed[BLK : BLK + 1], value

    span = rows + gcount

    def global_part(l):
        tops, totals, parts = [], [], []
        for p in range(pairs):
            top, total, value = attend(l, p, 2, k_own, v_own, 0, span)
            for lanes in (slice(0, BLK), slice(BLK, wide)):
                tops.append(top[:, lanes])
                totals.append(total[:, lanes])
                parts.append(value[:, lanes])
        stats = three_parts(jnp.concatenate(tops, axis=0)) + three_parts(jnp.concatenate(totals, axis=0))
        pad = jnp.zeros((BLK - 6 * heads, BLK), F32)
        packed = jnp.transpose(jnp.concatenate(parts + list(stats) + [pad], axis=0))
        half = width // 2
        tail = packed[:, width:]
        upper = jnp.concatenate([packed[:, :half], tail], axis=1)
        lower = jnp.concatenate([packed[:, half:width], tail], axis=1)
        for o in range(owners):
            cut = slice(o * GROWS, (o + 1) * GROWS)
            rs_src[l, o] = jnp.concatenate([upper[cut], lower[cut]], axis=0).astype(BF16)
        others(owners, lambda peer: rs_copy(l, peer, me).start())

    def combine(l):
        rs_buf[l, me] = rs_src[l, me]
        others(n, lambda peer: rs_copy(l, me, peer).wait_recv())
        half = width // 2
        got = rs_buf[l].astype(F32)
        upper = got[:, :GROWS, :]
        lower = got[:, GROWS:, :]
        stats = upper[:, :, half:].reshape(n * GROWS, BLK).astype(BF16)
        top = jnp.dot(stats, spread[0], preferred_element_type=F32).reshape(n, GROWS, width)
        total = jnp.dot(stats, spread[1], preferred_element_type=F32).reshape(n, GROWS, width)
        value = jnp.concatenate([upper[:, :, :half], lower[:, :, :half]], axis=2)
        factor = jnp.exp(top - jnp.max(top, axis=0, keepdims=True))
        mix = jnp.sum(value * factor, axis=0) / jnp.sum(total * factor, axis=0)
        mix = jnp.concatenate([mix, mix], axis=0).astype(BF16)
        new = gown[...] + jnp.dot(mix, wout[l], preferred_element_type=F32)[:GROWS]
        gown[...] = new
        if l + 1 < LAYERS:
            new = norm_rows(new, gg_ref[l + 1 : l + 2, :])
        ag_buf[l, me] = fold(new).astype(BF16)
        others(n, lambda peer: ag_copy(l, peer, me).start())

    def gathered(l):
        others(owners, lambda peer: ag_copy(l, me, peer).wait_recv())
        got = ag_buf[l].astype(F32)
        half = width // 2
        return jnp.concatenate(
            [got[:, :GROWS].reshape(gcount, half), got[:, GROWS:].reshape(gcount, half)], axis=1
        ).astype(BF16)

    def near_part(l):
        for rb in range(2):
            for p in range(pairs):
                top, total, value = attend(l, p, rb, k_own, v_own, 0, rows)
                m_a[rb, p] = top
                l_a[rb, p] = total
                o_a[rb, p] = value

    for l in range(LAYERS):
        if l == 0:
            w_in[0].wait()
            project_global(0)
            project_local(0)
            global_part(0)
            near_part(0)
            wout_in.wait()
        else:
            w_in[l].wait()
            project_local(l)
            near_part(l)
            xa[l, rows:span, :] = gathered(l - 1)
            project_global(l)
            global_part(l)

        wait_halo(l)
        if l == 0:
            @pl.when(has_left)
            def _():
                seg_to_right().wait_recv()

            @pl.when(has_right)
            def _():
                seg_to_left().wait_recv()

            for side in range(2):
                for part in range(2):
                    put_marks(
                        k_far, side * span + part * BLK, marks(seg_halo[side, part : part + 1, :])
                    )

        put_keys(l, xh[l, 0:rows, :], (k_far, v_far, 0))
        put_keys(l, xh[l, rows : 2 * rows, :], (k_far, v_far, span))
        only_owner(functools.partial(combine, l))

        for rb in range(2):
            for p in range(pairs):
                top_b, total_b, value_b = attend(
                    l, p, rb, k_far, v_far, rb * BLK, 4 * BLK, masked=True
                )
                top_a = m_a[rb, p]
                top = jnp.maximum(top_a, top_b)
                fa = jnp.exp(top_a - top)
                fb = jnp.exp(top_b - top)
                inv = 1.0 / (l_a[rb, p] * fa + total_b * fb)
                value = o_a[rb, p] * (fa * inv) + value_b * (fb * inv)
                lanes = slice(rb * BLK, (rb + 1) * BLK)
                mixt[p * BLK : p * BLK + head_dim, lanes] = value[:, :BLK]
                mixt[p * BLK + head_dim : (p + 1) * BLK, lanes] = value[:, BLK:]

        mix = jnp.transpose(mixt[...]).astype(BF16)
        new = stream[...] + jnp.dot(mix, wout[l], preferred_element_type=F32)
        if l + 1 < LAYERS:
            stream[...] = new
            xa[l + 1, 0:rows, :] = norm_rows(new, gl_ref[l + 1 : l + 2, :]).astype(BF16)
            send_halo(l + 1)
        else:
            out_ref[...] = new.astype(BF16)

    gout_ref[...] = gathered(LAYERS - 1)

    @pl.when(has_right)
    def _():
        seg_to_right().wait_send()
        for l in range(LAYERS):
            halo_to_right(l).wait_send()

    @pl.when(has_left)
    def _():
        seg_to_left().wait_send()
        for l in range(LAYERS):
            halo_to_left(l).wait_send()

    for l in range(LAYERS):
        others(owners, lambda peer: rs_copy(l, peer, me).wait_send())
        only_owner(lambda: others(n, lambda peer: ag_copy(l, peer, me).wait_send()))


def per_device(n, tokens, globals_in, seg_ids, table, w_qkv, w_out, gain_local, gain_global, seg_bias):
    rows, width = tokens.shape
    gcount = globals_in.shape[0]
    heads = seg_bias.shape[1]
    assert rows == 2 * BLK and gcount == BLK and heads == 8
    owners = min(n, gcount // GROWS)
    assert owners * GROWS == gcount
    span = rows + gcount
    vmem = pl.BlockSpec(memory_space=pltpu.VMEM)
    hbm = pl.BlockSpec(memory_space=pltpu.HBM)
    dma = pltpu.SemaphoreType.DMA
    V = pltpu.VMEM
    half = width // 2
    pairs, wide, head_dim = heads // 2, 2 * BLK, width // heads
    assert 2 * head_dim == BLK
    return pl.pallas_call(
        functools.partial(kernel, n, owners, heads),
        out_shape=(
            jax.ShapeDtypeStruct((rows, width), BF16),
            jax.ShapeDtypeStruct((gcount, width), BF16),
        ),
        in_specs=[hbm] * 9,
        out_specs=(vmem, vmem),
        scratch_shapes=[
            V((rows, width), BF16),
            V((gcount, width), BF16),
            V((2, BLK), jnp.int32),
            V((1, BLK), jnp.int32),
            V((LAYERS, width, 3 * width), BF16),
            V((LAYERS, width, width), BF16),
            V((LAYERS, width), F32),
            V((LAYERS, width), F32),
            V((LAYERS, heads), F32),
            V((LAYERS, span, width), BF16),
            V((LAYERS, 2 * rows, width), BF16),
            V((8, BLK), F32),
            V((2, 8, BLK), F32),
            V((LAYERS, pairs, 3, wide, wide), BF16),
            V((span, pairs * wide), BF16),
            V((pairs, BLK + ONES, span), BF16),
            V((2 * rows + gcount, pairs * wide), BF16),
            V((pairs, BLK + ONES, 2 * rows + gcount), BF16),
            V((2, BLK, wide), F32),
            V((2, BLK, width), BF16),
            V((2, pairs, head_dim, wide), F32),
            V((2, pairs, 1, wide), F32),
            V((2, pairs, 1, wide), F32),
            V((width, rows), F32),
            V((rows, width), F32),
            V((gcount, width), F32),
            V((GROWS, width), F32),
            V((LAYERS, owners, 2 * GROWS, half + BLK), BF16),
            V((LAYERS, n, 2 * GROWS, half + BLK), BF16),
            V((LAYERS, owners, 2 * GROWS, half), BF16),
            dma((8 + LAYERS,)),
            dma((2,)),
            dma((2,)),
            dma((LAYERS, 2)),
            dma((LAYERS, 2)),
            dma((LAYERS, owners)),
            dma((LAYERS, n)),
            dma((LAYERS, n)),
            dma((LAYERS, owners)),
        ],
        compiler_params=pltpu.CompilerParams(
            collective_id=0, has_side_effects=True, vmem_limit_bytes=VMEM_BYTES
        ),
        name="encoder",
    )(
        tokens, globals_in, seg_ids.reshape(2, BLK), table.reshape(1, BLK),
        w_qkv, w_out, gain_local, gain_global, seg_bias,
    )


def solution(mesh):
    return jax.shard_map(
        functools.partial(per_device, mesh.shape["seq"]),
        mesh=mesh,
        in_specs=(
            P(("dp", "seq"), None),
            P("dp", None),
            P(("dp", "seq")),
            P("dp"),
            P(),
            P(),
            P(),
            P(),
            P(),
        ),
        out_specs=(P(("dp", "seq"), None), P("dp", None)),
        check_vma=False,
    )
```

```python
import functools

import jax
import jax.numpy as jnp
from jax import lax
from jax.experimental import pallas as pl
from jax.experimental.pallas import tpu as pltpu
from jax.sharding import PartitionSpec as P

LAYERS = 2
BLK = 128
GROWS = 8
IDS = 64
ONES = 16
VMEM_BYTES = 62 * 1024 * 1024
NEG = -1e30
F32 = jnp.float32
BF16 = jnp.bfloat16


def norm_rows(values, gain):
    average = jnp.mean(values, axis=-1, keepdims=True)
    centered = values - average
    variance = jnp.mean(centered * centered, axis=-1, keepdims=True)
    return centered * lax.rsqrt(variance + 1e-05) * gain


def three_parts(x):
    hi = x.astype(BF16).astype(F32)
    rest = x - hi
    mid = rest.astype(BF16).astype(F32)
    return hi, mid, (rest - mid).astype(BF16).astype(F32)


def fold(rows):
    half = rows.shape[1] // 2
    return jnp.concatenate([rows[:, :half], rows[:, half:]], axis=0)


def steps(first, last, body):
    if last <= 16:
        for i in range(first, last):
            body(i)
    else:
        pl.loop(first, last)(body)


def kernel(
    n, owners, heads,
    tok_hbm, glob_hbm, seg_hbm, table_hbm, wqkv_hbm, wout_hbm, gl_hbm, gg_hbm, bias_hbm,
    out_ref, gout_ref,
    tok_ref, glob_ref, seg_ref, table_ref, wqkv, wout, gl_ref, gg_ref, bias_ref,
    xa, xh, seg_own, seg_halo,
    qs, k_own, v_own, k_far, v_far, tri, spread,
    o_a, m_a, l_a, mixt, stream, gall, gown, rs_src, rs_buf, ag_buf,
    in_sem, seg_send, seg_recv, h_send, h_recv, rs_send, rs_recv, ag_send, ag_recv,
):
    rows, width = tok_ref.shape
    gcount = glob_ref.shape[0]
    head_dim = width // heads
    me = lax.axis_index("seq")
    has_left = me > 0
    has_right = me < n - 1
    left = jnp.maximum(me - 1, 0)
    right = jnp.minimum(me + 1, n - 1)

    barrier = pltpu.get_barrier_semaphore()

    each_peer = functools.partial(steps, 1, n)

    @each_peer
    def _(r):
        pl.semaphore_signal(
            barrier, inc=1, device_id={"seq": lax.rem(me + r, n)},
            device_id_type=pl.DeviceIdType.MESH,
        )

    def load(i, src, dst):
        copy = pltpu.make_async_copy(src, dst, in_sem.at[i])
        copy.start()
        return copy

    tok_in = load(0, tok_hbm, tok_ref)
    gl_in = load(1, gl_hbm, gl_ref)
    seg_in = load(2, seg_hbm, seg_ref)
    w_in = [load(3, wqkv_hbm.at[0], wqkv.at[0])]
    small_in = [
        load(4, glob_hbm, glob_ref),
        load(5, table_hbm, table_ref),
        load(6, gg_hbm, gg_ref),
        load(7, bias_hbm, bias_ref),
    ]
    wout_in = load(8, wout_hbm, wout)
    w_in += [load(8 + l, wqkv_hbm.at[l], wqkv.at[l]) for l in range(1, LAYERS)]

    pairs = heads // 2
    wide = 2 * BLK
    seg_in.wait()
    seg_own[...] = jnp.zeros(seg_own.shape, F32)
    seg_own[0:2, :] = seg_ref[...].astype(F32)

    @pl.when(jnp.logical_not(has_left))
    def _():
        seg_halo[0] = jnp.zeros(seg_halo.shape[1:], F32)
        for l in range(LAYERS):
            xh[l, 0:rows, :] = jnp.zeros((rows, width), BF16)

    @pl.when(jnp.logical_not(has_right))
    def _():
        seg_halo[1] = jnp.zeros(seg_halo.shape[1:], F32)
        for l in range(LAYERS):
            xh[l, rows : 2 * rows, :] = jnp.zeros((rows, width), BF16)

    tok_in.wait()
    gl_in.wait()
    stream[...] = tok_ref[...].astype(F32)
    xa[0, 0:rows, :] = norm_rows(stream[...], gl_ref[0:1, :]).astype(BF16)
    pl.semaphore_wait(barrier, n - 1)

    def remote(src, dst, ssem, rsem, target):
        return pltpu.make_async_remote_copy(
            src_ref=src, dst_ref=dst, send_sem=ssem, recv_sem=rsem,
            device_id={"seq": target}, device_id_type=pl.DeviceIdType.MESH,
        )

    def halo_to_right(l, c):
        piece = pl.ds(c * BLK, BLK)
        return remote(xa.at[l, piece], xh.at[l, piece], h_send.at[l, 0, c], h_recv.at[l, 0, c], right)

    def halo_to_left(l, c):
        return remote(
            xa.at[l, pl.ds(c * BLK, BLK)], xh.at[l, pl.ds(rows + c * BLK, BLK)],
            h_send.at[l, 1, c], h_recv.at[l, 1, c], left,
        )

    def seg_to_right():
        return remote(seg_own, seg_halo.at[0], seg_send.at[0], seg_recv.at[0], right)

    def seg_to_left():
        return remote(seg_own, seg_halo.at[1], seg_send.at[1], seg_recv.at[1], left)

    def send_halo(l, c):
        @pl.when(has_right)
        def _():
            halo_to_right(l, c).start()

        @pl.when(has_left)
        def _():
            halo_to_left(l, c).start()

    def wait_left(l):
        @pl.when(has_left)
        def _():
            for c in range(2):
                halo_to_right(l, c).wait_recv()

    def wait_right(l):
        @pl.when(has_right)
        def _():
            for c in range(2):
                halo_to_left(l, c).wait_recv()

    for c in range(2):
        send_halo(0, c)

    @pl.when(has_right)
    def _():
        seg_to_right().start()

    @pl.when(has_left)
    def _():
        seg_to_left().start()

    all_own = n == owners

    def only_owner(body):
        if all_own:
            body()
        else:
            pl.when(me < owners)(body)

    def rs_copy(l, target, slot):
        return remote(
            rs_src.at[l, target], rs_buf.at[l, slot], rs_send.at[l], rs_recv.at[l], target
        )

    def rs_start(l):
        def send(r):
            target = lax.rem(me + r, n)
            if all_own:
                rs_copy(l, target, r - 1).start()
            else:
                @pl.when(target < owners)
                def _():
                    rs_copy(l, target, r - 1).start()

        steps(1, n, send)

    def ag_start(l):
        def send(r):
            mine = ag_buf.at[l, me]
            remote(mine, mine, ag_send.at[l], ag_recv.at[l], lax.rem(me + r, n)).start()

        steps(1, n, send)

    def drain(ref, sem):
        pltpu.make_async_copy(ref, ref, sem).wait()

    def drain_sent(l):
        for first in range(0, n - 1, owners):
            drain(ag_buf.at[l, pl.ds(0, min(owners, n - 1 - first))], ag_send.at[l])

    def by_owner(body):
        if all_own:
            body(owners - 1)
        else:
            pl.when(me < owners)(lambda: body(owners - 1))
            pl.when(me >= owners)(lambda: body(owners))

    for copy in small_in:
        copy.wait()

    xa[0, rows : rows + gcount, :] = norm_rows(glob_ref[...].astype(F32), gg_ref[0:1, :]).astype(BF16)
    gall[...] = glob_ref[...].astype(F32)

    def take_own():
        gown[...] = gall[pl.ds(me * GROWS, GROWS), :]

    only_owner(take_own)

    lane = lax.broadcasted_iota(jnp.int32, (BLK, BLK), 1)
    lane_idf = (lane & (IDS - 1)).astype(F32)
    deep = lax.broadcasted_iota(jnp.int32, (BLK, BLK), 0)
    deep_idf = (deep & (IDS - 1)).astype(F32)
    low = deep < IDS

    def down(row):
        return jnp.transpose(jnp.broadcast_to(row, (BLK, BLK)))

    def marks(row):
        return jnp.where(down(row) == lane_idf, 1.0, 0.0).astype(F32)

    def put_marks(ref, at, value):
        for p in range(pairs):
            ref[at : at + BLK, p * wide + BLK : (p + 1) * wide] = value.astype(BF16)

    for l in range(LAYERS):
        for p in range(pairs):
            for b in range(3):
                qs[l, p, b, 0:BLK, :] = jnp.zeros((BLK, wide), BF16)

    outside = jnp.where(deep == 0, NEG, 0.0).astype(F32)
    for rb in range(2):
        row = seg_own[rb : rb + 1, :]
        put_marks(k_own, rb * BLK, marks(row))
        own = jnp.where(jnp.broadcast_to(row, (BLK, BLK)) == deep_idf, 1.0, 0.0).astype(F32)
        for l in range(LAYERS):
            for h in range(heads):
                b = jnp.broadcast_to(bias_ref[l : l + 1, h : h + 1], (BLK, BLK))
                b_hi = b.astype(BF16).astype(F32)
                qs[l, h // 2, rb, BLK:, (h % 2) * BLK : (h % 2 + 1) * BLK] = (
                    own * jnp.where(low, b_hi, b - b_hi) + outside
                ).astype(BF16)
    hidden = jnp.where(me == 0, 0.0, 1.0).astype(F32)
    g_marks = jnp.where(lane == IDS, 1.0, 0.0).astype(F32) * hidden
    put_marks(k_own, rows, g_marks)
    put_marks(k_far, rows, g_marks)
    member = jnp.broadcast_to(table_ref[...].astype(F32), (BLK, BLK)) == deep_idf
    g_side = jnp.where((low & (deep > 0) & jnp.logical_not(member)) | (deep == IDS), NEG, 0.0)
    g_side = g_side.astype(F32).astype(BF16)
    for l in range(LAYERS):
        for p in range(pairs):
            qs[l, p, 2, BLK:, 0:BLK] = g_side
            qs[l, p, 2, BLK:, BLK:] = g_side

    tr = lax.broadcasted_iota(jnp.int32, (BLK, wide), 0)
    tc = lax.broadcasted_iota(jnp.int32, (BLK, wide), 1) & (BLK - 1)
    tri[0] = jnp.where(tr >= tc, 0.0, NEG).astype(F32)
    tri[1] = jnp.where(tr <= tc, 0.0, NEG).astype(F32)
    v_own[:, BLK:, :] = jnp.ones((pairs, ONES, rows + gcount), BF16)
    v_far[:, BLK:, :] = jnp.ones((pairs, ONES, 2 * rows + gcount), BF16)

    pick = lax.broadcasted_iota(jnp.int32, (BLK, width), 0)
    start = lax.broadcasted_iota(jnp.int32, (BLK, width), 1) & (head_dim - 1)
    head_of = (lax.broadcasted_iota(jnp.int32, (BLK, width), 1) - start).astype(F32) * (1.0 / head_dim)
    pick_head = (pick & 7).astype(F32)
    for i in range(2):
        hit = (pick_head == head_of) & (pick >= 24 * i) & (pick < 24 * (i + 1))
        spread[i] = jnp.where(hit, 1.0, 0.0).astype(F32).astype(BF16)

    def put_keys(l, x, *places):
        count = x.shape[0]
        k = jnp.dot(x, wqkv[l, :, width : 2 * width], preferred_element_type=F32).astype(BF16)
        v = jnp.dot(x, wqkv[l, :, 2 * width : 3 * width], preferred_element_type=F32).astype(BF16)
        v = jnp.transpose(v)
        for k_ref, v_ref, at in places:
            for p in range(pairs):
                k_ref[at : at + count, p * wide : p * wide + BLK] = k[:, p * BLK : (p + 1) * BLK]
                v_ref[p, 0:BLK, at : at + count] = v[p * BLK : (p + 1) * BLK]

    def put_queries(l, x, first):
        q = jnp.dot(x, wqkv[l, :, 0:width], preferred_element_type=F32)
        q = jnp.transpose((q * 0.125).astype(BF16))
        for b in range(x.shape[0] // BLK):
            for p in range(pairs):
                lanes = slice(b * BLK, (b + 1) * BLK)
                at = p * BLK
                qs[l, p, first + b, 0:head_dim, 0:BLK] = q[at : at + head_dim, lanes]
                qs[l, p, first + b, head_dim:BLK, BLK:] = q[at + head_dim : at + BLK, lanes]

    def project_local(l):
        x = xa[l, 0:rows, :]
        put_queries(l, x, 0)
        put_keys(l, x, (k_own, v_own, 0))

    def project_global(l):
        x = xa[l, rows : rows + gcount, :]
        put_queries(l, x, 2)
        put_keys(l, x, (k_own, v_own, rows), (k_far, v_far, rows))

    def attend(l, p, rb, k_ref, v_ref, k0, count, masked=False):
        s = jnp.dot(
            k_ref[k0 : k0 + count, p * wide : (p + 1) * wide], qs[l, p, rb],
            preferred_element_type=F32,
        )
        if masked:
            s = jnp.concatenate(
                [s[:BLK] + tri[0], s[BLK : count - BLK], s[count - BLK :] + tri[1]], axis=0
            )
        top = jnp.max(s, axis=0, keepdims=True)
        probs = jnp.exp(s - top).astype(BF16)
        mixed = jnp.dot(v_ref[p, :, k0 : k0 + count], probs, preferred_element_type=F32)
        value = jnp.concatenate([mixed[:head_dim, :BLK], mixed[head_dim:BLK, BLK:]], axis=1)
        return top, mixed[BLK : BLK + 1], value

    span = rows + gcount

    def global_part(l):
        tops, totals, parts = [], [], []
        for p in range(pairs):
            top, total, value = attend(l, p, 2, k_own, v_own, 0, span)
            for lanes in (slice(0, BLK), slice(BLK, wide)):
                tops.append(top[:, lanes])
                totals.append(total[:, lanes])
                parts.append(value[:, lanes])
        stats = three_parts(jnp.concatenate(tops, axis=0)) + three_parts(jnp.concatenate(totals, axis=0))
        pad = jnp.zeros((BLK - 6 * heads, BLK), F32)
        packed = jnp.transpose(jnp.concatenate(parts + list(stats) + [pad], axis=0))
        half = width // 2
        tail = packed[:, width:]
        upper = jnp.concatenate([packed[:, :half], tail], axis=1)
        lower = jnp.concatenate([packed[:, half:width], tail], axis=1)
        for o in range(owners):
            cut = slice(o * GROWS, (o + 1) * GROWS)
            rs_src[l, o] = jnp.concatenate([upper[cut], lower[cut]], axis=0).astype(BF16)
        rs_start(l)

    def combine(l):
        rs_buf[l, n - 1] = rs_src[l, me]
        drain(rs_buf.at[l, pl.ds(0, n - 1)], rs_recv.at[l])
        half = width // 2
        got = rs_buf[l].astype(F32)
        upper = got[:, :GROWS, :]
        lower = got[:, GROWS:, :]
        stats = upper[:, :, half:].reshape(n * GROWS, BLK).astype(BF16)
        top = jnp.dot(stats, spread[0], preferred_element_type=F32).reshape(n, GROWS, width)
        total = jnp.dot(stats, spread[1], preferred_element_type=F32).reshape(n, GROWS, width)
        value = jnp.concatenate([upper[:, :, :half], lower[:, :, :half]], axis=2)
        factor = jnp.exp(top - jnp.max(top, axis=0, keepdims=True))
        mix = jnp.sum(value * factor, axis=0) / jnp.sum(total * factor, axis=0)
        mix = jnp.concatenate([mix, mix], axis=0).astype(BF16)
        new = gown[...] + jnp.dot(mix, wout[l], preferred_element_type=F32)[:GROWS]
        gown[...] = new
        if l + 1 < LAYERS:
            new = norm_rows(new, gg_ref[l + 1 : l + 2, :])
        ag_buf[l, me] = fold(new).astype(BF16)
        ag_start(l)

    def gathered(l):
        by_owner(lambda slots: drain(ag_buf.at[l, pl.ds(0, slots)], ag_recv.at[l]))
        got = ag_buf[l].astype(F32)
        half = width // 2
        return jnp.concatenate(
            [got[:, :GROWS].reshape(gcount, half), got[:, GROWS:].reshape(gcount, half)], axis=1
        ).astype(BF16)

    def near_part(l):
        for rb in range(2):
            for p in range(pairs):
                top, total, value = attend(l, p, rb, k_own, v_own, 0, rows)
                m_a[rb, p] = top
                l_a[rb, p] = total
                o_a[rb, p] = value

    for l in range(LAYERS):
        if l == 0:
            w_in[0].wait()
            project_global(0)
            project_local(0)
            global_part(0)
            near_part(0)
            wout_in.wait()
        else:
            w_in[l].wait()
            project_local(l)
            near_part(l)
            xa[l, rows:span, :] = gathered(l - 1)
            project_global(l)
            global_part(l)

        if l == 0:
            @pl.when(has_left)
            def _():
                seg_to_right().wait_recv()

            @pl.when(has_right)
            def _():
                seg_to_left().wait_recv()

            for side in range(2):
                for part in range(2):
                    put_marks(
                        k_far, side * span + part * BLK, marks(seg_halo[side, part : part + 1, :])
                    )

        wait_left(l)
        put_keys(l, xh[l, 0:rows, :], (k_far, v_far, 0))
        wait_right(l)
        put_keys(l, xh[l, rows : 2 * rows, :], (k_far, v_far, span))
        only_owner(functools.partial(combine, l))

        for rb in range(2):
            for p in range(pairs):
                top_b, total_b, value_b = attend(
                    l, p, rb, k_far, v_far, rb * BLK, 4 * BLK, masked=True
                )
                top_a = m_a[rb, p]
                top = jnp.maximum(top_a, top_b)
                fa = jnp.exp(top_a - top)
                fb = jnp.exp(top_b - top)
                inv = 1.0 / (l_a[rb, p] * fa + total_b * fb)
                value = o_a[rb, p] * (fa * inv) + value_b * (fb * inv)
                mixt[rb, p * BLK : p * BLK + head_dim, :] = value[:, :BLK]
                mixt[rb, p * BLK + head_dim : (p + 1) * BLK, :] = value[:, BLK:]

            here = slice(rb * BLK, (rb + 1) * BLK)
            mix = jnp.transpose(mixt[rb].astype(BF16))
            new = stream[here, :] + jnp.dot(mix, wout[l], preferred_element_type=F32)
            if l + 1 < LAYERS:
                stream[here, :] = new
                xa[l + 1, here, :] = norm_rows(new, gl_ref[l + 1 : l + 2, :]).astype(BF16)
                send_halo(l + 1, rb)
            else:
                out_ref[here, :] = new.astype(BF16)

    gout_ref[...] = gathered(LAYERS - 1)

    @pl.when(has_right)
    def _():
        seg_to_right().wait_send()
        for l in range(LAYERS):
            for c in range(2):
                halo_to_right(l, c).wait_send()

    @pl.when(has_left)
    def _():
        seg_to_left().wait_send()
        for l in range(LAYERS):
            for c in range(2):
                halo_to_left(l, c).wait_send()

    for l in range(LAYERS):
        by_owner(lambda slots: drain(rs_src.at[l, pl.ds(0, slots)], rs_send.at[l]))
        only_owner(lambda: drain_sent(l))


def hand_on(a_ref, b_ref, a_out, b_out, sems):
    half = a_ref.shape[0] // 2
    copies = [
        pltpu.make_async_copy(a_ref.at[pl.ds(0, half)], a_out.at[pl.ds(0, half)], sems.at[0]),
        pltpu.make_async_copy(a_ref.at[pl.ds(half, half)], a_out.at[pl.ds(half, half)], sems.at[1]),
        pltpu.make_async_copy(b_ref, b_out, sems.at[2]),
    ]
    for copy in copies:
        copy.start()
    for copy in copies:
        copy.wait()


def per_device(n, tokens, globals_in, seg_ids, table, w_qkv, w_out, gain_local, gain_global, seg_bias):
    rows, width = tokens.shape
    gcount = globals_in.shape[0]
    heads = seg_bias.shape[1]
    assert rows == 2 * BLK and gcount == BLK and heads == 8
    owners = min(n, gcount // GROWS)
    assert owners * GROWS == gcount
    span = rows + gcount
    vmem = pl.BlockSpec(memory_space=pltpu.VMEM)
    hbm = pl.BlockSpec(memory_space=pltpu.HBM)
    dma = pltpu.SemaphoreType.DMA
    V = pltpu.VMEM
    half = width // 2
    pairs, wide, head_dim = heads // 2, 2 * BLK, width // heads
    assert 2 * head_dim == BLK
    local, shared = pl.pallas_call(
        functools.partial(kernel, n, owners, heads),
        out_shape=(
            jax.ShapeDtypeStruct((rows, width), BF16),
            jax.ShapeDtypeStruct((gcount, width), BF16),
        ),
        in_specs=[hbm] * 9,
        out_specs=(vmem, vmem),
        scratch_shapes=[
            V((rows, width), BF16),
            V((gcount, width), BF16),
            V((2, BLK), jnp.int32),
            V((1, BLK), jnp.int32),
            V((LAYERS, width, 3 * width), BF16),
            V((LAYERS, width, width), BF16),
            V((LAYERS, width), F32),
            V((LAYERS, width), F32),
            V((LAYERS, heads), F32),
            V((LAYERS, span, width), BF16),
            V((LAYERS, 2 * rows, width), BF16),
            V((8, BLK), F32),
            V((2, 8, BLK), F32),
            V((LAYERS, pairs, 3, wide, wide), BF16),
            V((span, pairs * wide), BF16),
            V((pairs, BLK + ONES, span), BF16),
            V((2 * rows + gcount, pairs * wide), BF16),
            V((pairs, BLK + ONES, 2 * rows + gcount), BF16),
            V((2, BLK, wide), F32),
            V((2, BLK, width), BF16),
            V((2, pairs, head_dim, wide), F32),
            V((2, pairs, 1, wide), F32),
            V((2, pairs, 1, wide), F32),
            V((2, width, BLK), F32),
            V((rows, width), F32),
            V((gcount, width), F32),
            V((GROWS, width), F32),
            V((LAYERS, owners, 2 * GROWS, half + BLK), BF16),
            V((LAYERS, n, 2 * GROWS, half + BLK), BF16),
            V((LAYERS, owners, 2 * GROWS, half), BF16),
            dma((8 + LAYERS,)),
            dma((2,)),
            dma((2,)),
            dma((LAYERS, 2, 2)),
            dma((LAYERS, 2, 2)),
            dma((LAYERS,)),
            dma((LAYERS,)),
            dma((LAYERS,)),
            dma((LAYERS,)),
        ],
        compiler_params=pltpu.CompilerParams(
            collective_id=0, has_side_effects=True, vmem_limit_bytes=VMEM_BYTES
        ),
        name="encoder",
    )(
        tokens, globals_in, seg_ids.reshape(2, BLK), table.reshape(1, BLK),
        w_qkv, w_out, gain_local, gain_global, seg_bias,
    )
    return pl.pallas_call(
        hand_on,
        out_shape=(
            jax.ShapeDtypeStruct(local.shape, BF16),
            jax.ShapeDtypeStruct(shared.shape, BF16),
        ),
        in_specs=[hbm, hbm],
        out_specs=(hbm, hbm),
        scratch_shapes=[dma((3,))],
        compiler_params=pltpu.CompilerParams(vmem_limit_bytes=VMEM_BYTES),
        name="hand_on",
    )(local, shared)


def solution(mesh):
    return jax.shard_map(
        functools.partial(per_device, mesh.shape["seq"]),
        mesh=mesh,
        in_specs=(
            P(("dp", "seq"), None),
            P("dp", None),
            P(("dp", "seq")),
            P("dp"),
            P(),
            P(),
            P(),
            P(),
            P(),
        ),
        out_specs=(P(("dp", "seq"), None), P("dp", None)),
        check_vma=False,
    )
```

```python
import functools

import jax
import jax.numpy as jnp
from jax import lax
from jax.experimental import pallas as pl
from jax.experimental.pallas import tpu as pltpu
from jax.sharding import PartitionSpec as P

LAYERS = 2
BLK = 128
GROWS = 8
IDS = 64
ONES = 16
VMEM_BYTES = 62 * 1024 * 1024
NEG = -1e30
F32 = jnp.float32
BF16 = jnp.bfloat16


def norm_rows(values, gain):
    average = jnp.mean(values, axis=-1, keepdims=True)
    centered = values - average
    variance = jnp.mean(centered * centered, axis=-1, keepdims=True)
    return centered * lax.rsqrt(variance + 1e-05) * gain


def three_parts(x):
    hi = x.astype(BF16).astype(F32)
    rest = x - hi
    mid = rest.astype(BF16).astype(F32)
    return hi, mid, (rest - mid).astype(BF16).astype(F32)


def fold(rows):
    half = rows.shape[1] // 2
    return jnp.concatenate([rows[:, :half], rows[:, half:]], axis=0)


def steps(first, last, body):
    if last <= 16:
        for i in range(first, last):
            body(i)
    else:
        pl.loop(first, last)(body)


def kernel(
    n, owners, heads,
    tok_hbm, glob_hbm, seg_hbm, table_hbm, wqkv_hbm, wout_hbm, gl_hbm, gg_hbm, bias_hbm,
    out_ref, gout_ref,
    tok_ref, glob_ref, seg_ref, table_ref, wqkv, wout, gl_ref, gg_ref, bias_ref,
    xa, xh, seg_own, seg_halo,
    qs, k_own, v_own, k_far, v_far, tri, spread,
    o_a, m_a, l_a, mixt, stream, gall, gown, rs_src, rs_buf, ag_buf,
    in_sem, seg_send, seg_recv, h_send, h_recv, rs_send, rs_recv, ag_send, ag_recv,
):
    rows, width = tok_ref.shape
    gcount = glob_ref.shape[0]
    head_dim = width // heads
    me = lax.axis_index("seq")
    has_left = me > 0
    has_right = me < n - 1
    left = jnp.maximum(me - 1, 0)
    right = jnp.minimum(me + 1, n - 1)

    barrier = pltpu.get_barrier_semaphore()

    each_peer = functools.partial(steps, 1, n)

    @each_peer
    def _(r):
        pl.semaphore_signal(
            barrier, inc=1, device_id={"seq": lax.rem(me + r, n)},
            device_id_type=pl.DeviceIdType.MESH,
        )

    def load(i, src, dst):
        copy = pltpu.make_async_copy(src, dst, in_sem.at[i])
        copy.start()
        return copy

    tok_in = load(0, tok_hbm, tok_ref)
    gl_in = load(1, gl_hbm, gl_ref)
    seg_in = load(2, seg_hbm, seg_ref)
    w_in = [load(3, wqkv_hbm.at[0], wqkv.at[0])]
    small_in = [
        load(4, glob_hbm, glob_ref),
        load(5, table_hbm, table_ref),
        load(6, gg_hbm, gg_ref),
        load(7, bias_hbm, bias_ref),
    ]
    wout_in = load(8, wout_hbm, wout)
    w_in += [load(8 + l, wqkv_hbm.at[l], wqkv.at[l]) for l in range(1, LAYERS)]

    pairs = heads // 2
    wide = 2 * BLK
    seg_in.wait()
    seg_own[...] = jnp.zeros(seg_own.shape, F32)
    seg_own[0:2, :] = seg_ref[...].astype(F32)

    @pl.when(jnp.logical_not(has_left))
    def _():
        seg_halo[0] = jnp.zeros(seg_halo.shape[1:], F32)
        for l in range(LAYERS):
            xh[l, 0:rows, :] = jnp.zeros((rows, width), BF16)

    @pl.when(jnp.logical_not(has_right))
    def _():
        seg_halo[1] = jnp.zeros(seg_halo.shape[1:], F32)
        for l in range(LAYERS):
            xh[l, rows : 2 * rows, :] = jnp.zeros((rows, width), BF16)

    tok_in.wait()
    gl_in.wait()
    stream[...] = tok_ref[...].astype(F32)
    xa[0, 0:rows, :] = norm_rows(stream[...], gl_ref[0:1, :]).astype(BF16)
    pl.semaphore_wait(barrier, n - 1)

    def remote(src, dst, ssem, rsem, target):
        return pltpu.make_async_remote_copy(
            src_ref=src, dst_ref=dst, send_sem=ssem, recv_sem=rsem,
            device_id={"seq": target}, device_id_type=pl.DeviceIdType.MESH,
        )

    def halo_to_right(l, c):
        piece = pl.ds(c * BLK, BLK)
        return remote(xa.at[l, piece], xh.at[l, piece], h_send.at[l, 0, c], h_recv.at[l, 0, c], right)

    def halo_to_left(l, c):
        return remote(
            xa.at[l, pl.ds(c * BLK, BLK)], xh.at[l, pl.ds(rows + c * BLK, BLK)],
            h_send.at[l, 1, c], h_recv.at[l, 1, c], left,
        )

    def seg_to_right():
        return remote(seg_own, seg_halo.at[0], seg_send.at[0], seg_recv.at[0], right)

    def seg_to_left():
        return remote(seg_own, seg_halo.at[1], seg_send.at[1], seg_recv.at[1], left)

    def send_halo(l, c):
        @pl.when(has_right)
        def _():
            halo_to_right(l, c).start()

        @pl.when(has_left)
        def _():
            halo_to_left(l, c).start()

    def wait_left(l):
        @pl.when(has_left)
        def _():
            for c in range(2):
                halo_to_right(l, c).wait_recv()

    def wait_right(l):
        @pl.when(has_right)
        def _():
            for c in range(2):
                halo_to_left(l, c).wait_recv()

    for c in range(2):
        send_halo(0, c)

    @pl.when(has_right)
    def _():
        seg_to_right().start()

    @pl.when(has_left)
    def _():
        seg_to_left().start()

    all_own = n == owners

    def only_owner(body):
        if all_own:
            body()
        else:
            pl.when(me < owners)(body)

    def rs_copy(l, target, slot):
        return remote(
            rs_src.at[l, target], rs_buf.at[l, slot], rs_send.at[l], rs_recv.at[l], target
        )

    def rs_start(l):
        def send(r):
            target = lax.rem(me + r, n)
            if all_own:
                rs_copy(l, target, r - 1).start()
            else:
                @pl.when(target < owners)
                def _():
                    rs_copy(l, target, r - 1).start()

        steps(1, n, send)

    def ag_start(l):
        def send(r):
            mine = ag_buf.at[l, me]
            remote(mine, mine, ag_send.at[l], ag_recv.at[l], lax.rem(me + r, n)).start()

        steps(1, n, send)

    def drain(ref, sem):
        pltpu.make_async_copy(ref, ref, sem).wait()

    def drain_sent(l):
        for first in range(0, n - 1, owners):
            drain(ag_buf.at[l, pl.ds(0, min(owners, n - 1 - first))], ag_send.at[l])

    def by_owner(body):
        if all_own:
            body(owners - 1)
        else:
            pl.when(me < owners)(lambda: body(owners - 1))
            pl.when(me >= owners)(lambda: body(owners))

    for copy in small_in:
        copy.wait()

    xa[0, rows : rows + gcount, :] = norm_rows(glob_ref[...].astype(F32), gg_ref[0:1, :]).astype(BF16)
    gall[...] = glob_ref[...].astype(F32)

    def take_own():
        gown[...] = gall[pl.ds(me * GROWS, GROWS), :]

    only_owner(take_own)

    lane = lax.broadcasted_iota(jnp.int32, (BLK, BLK), 1)
    lane_idf = (lane & (IDS - 1)).astype(F32)
    deep = lax.broadcasted_iota(jnp.int32, (BLK, BLK), 0)
    deep_idf = (deep & (IDS - 1)).astype(F32)
    low = deep < IDS

    def down(row):
        return jnp.transpose(jnp.broadcast_to(row, (BLK, BLK)))

    def marks(row):
        return jnp.where(down(row) == lane_idf, 1.0, 0.0).astype(F32)

    def put_marks(ref, at, value):
        for p in range(pairs):
            ref[at : at + BLK, p * wide + BLK : (p + 1) * wide] = value.astype(BF16)

    for l in range(LAYERS):
        for p in range(pairs):
            for b in range(3):
                qs[l, p, b, 0:BLK, :] = jnp.zeros((BLK, wide), BF16)

    outside = jnp.where(deep == 0, NEG, 0.0).astype(F32)
    for rb in range(2):
        row = seg_own[rb : rb + 1, :]
        put_marks(k_own, rb * BLK, marks(row))
        own = jnp.where(jnp.broadcast_to(row, (BLK, BLK)) == deep_idf, 1.0, 0.0).astype(F32)
        for l in range(LAYERS):
            for h in range(heads):
                b = jnp.broadcast_to(bias_ref[l : l + 1, h : h + 1], (BLK, BLK))
                b_hi = b.astype(BF16).astype(F32)
                qs[l, h // 2, rb, BLK:, (h % 2) * BLK : (h % 2 + 1) * BLK] = (
                    own * jnp.where(low, b_hi, b - b_hi) + outside
                ).astype(BF16)
    hidden = jnp.where(me == 0, 0.0, 1.0).astype(F32)
    g_marks = jnp.where(lane == IDS, 1.0, 0.0).astype(F32) * hidden
    put_marks(k_own, rows, g_marks)
    put_marks(k_far, rows, g_marks)
    member = jnp.broadcast_to(table_ref[...].astype(F32), (BLK, BLK)) == deep_idf
    g_side = jnp.where((low & (deep > 0) & jnp.logical_not(member)) | (deep == IDS), NEG, 0.0)
    g_side = g_side.astype(F32).astype(BF16)
    for l in range(LAYERS):
        for p in range(pairs):
            qs[l, p, 2, BLK:, 0:BLK] = g_side
            qs[l, p, 2, BLK:, BLK:] = g_side

    tr = lax.broadcasted_iota(jnp.int32, (BLK, wide), 0)
    tc = lax.broadcasted_iota(jnp.int32, (BLK, wide), 1) & (BLK - 1)
    tri[0] = jnp.where(tr >= tc, 0.0, NEG).astype(F32)
    tri[1] = jnp.where(tr <= tc, 0.0, NEG).astype(F32)
    v_own[:, BLK:, :] = jnp.ones((pairs, ONES, rows + gcount), BF16)
    v_far[:, BLK:, :] = jnp.ones((pairs, ONES, 2 * rows + gcount), BF16)

    pick = lax.broadcasted_iota(jnp.int32, (BLK, width), 0)
    start = lax.broadcasted_iota(jnp.int32, (BLK, width), 1) & (head_dim - 1)
    head_of = (lax.broadcasted_iota(jnp.int32, (BLK, width), 1) - start).astype(F32) * (1.0 / head_dim)
    pick_head = (pick & 7).astype(F32)
    for i in range(2):
        hit = (pick_head == head_of) & (pick >= 24 * i) & (pick < 24 * (i + 1))
        spread[i] = jnp.where(hit, 1.0, 0.0).astype(F32).astype(BF16)

    def put_keys(l, x, *places):
        count = x.shape[0]
        k = jnp.dot(x, wqkv[l, :, width : 2 * width], preferred_element_type=F32).astype(BF16)
        v = jnp.dot(x, wqkv[l, :, 2 * width : 3 * width], preferred_element_type=F32).astype(BF16)
        v = jnp.transpose(v)
        for k_ref, v_ref, at in places:
            for p in range(pairs):
                k_ref[at : at + count, p * wide : p * wide + BLK] = k[:, p * BLK : (p + 1) * BLK]
                v_ref[p, 0:BLK, at : at + count] = v[p * BLK : (p + 1) * BLK]

    def put_queries(l, x, first):
        q = jnp.dot(x, wqkv[l, :, 0:width], preferred_element_type=F32)
        q = jnp.transpose((q * 0.125).astype(BF16))
        for b in range(x.shape[0] // BLK):
            for p in range(pairs):
                lanes = slice(b * BLK, (b + 1) * BLK)
                at = p * BLK
                qs[l, p, first + b, 0:head_dim, 0:BLK] = q[at : at + head_dim, lanes]
                qs[l, p, first + b, head_dim:BLK, BLK:] = q[at + head_dim : at + BLK, lanes]

    def project_local(l):
        x = xa[l, 0:rows, :]
        put_queries(l, x, 0)
        put_keys(l, x, (k_own, v_own, 0))

    def project_global(l):
        x = xa[l, rows : rows + gcount, :]
        put_queries(l, x, 2)
        put_keys(l, x, (k_own, v_own, rows), (k_far, v_far, rows))

    def attend(l, p, rb, k_ref, v_ref, k0, count, masked=False):
        s = jnp.dot(
            k_ref[k0 : k0 + count, p * wide : (p + 1) * wide], qs[l, p, rb],
            preferred_element_type=F32,
        )
        if masked:
            s = jnp.concatenate(
                [s[:BLK] + tri[0], s[BLK : count - BLK], s[count - BLK :] + tri[1]], axis=0
            )
        top = jnp.max(s, axis=0, keepdims=True)
        probs = jnp.exp(s - top).astype(BF16)
        mixed = jnp.dot(v_ref[p, :, k0 : k0 + count], probs, preferred_element_type=F32)
        value = jnp.concatenate([mixed[:head_dim, :BLK], mixed[head_dim:BLK, BLK:]], axis=1)
        return top, mixed[BLK : BLK + 1], value

    span = rows + gcount

    def global_part(l):
        tops, totals, parts = [], [], []
        for p in range(pairs):
            top, total, value = attend(l, p, 2, k_own, v_own, 0, span)
            for lanes in (slice(0, BLK), slice(BLK, wide)):
                tops.append(top[:, lanes])
                totals.append(total[:, lanes])
                parts.append(value[:, lanes])
        stats = three_parts(jnp.concatenate(tops, axis=0)) + three_parts(jnp.concatenate(totals, axis=0))
        pad = jnp.zeros((BLK - 6 * heads, BLK), F32)
        packed = jnp.transpose(jnp.concatenate(parts + list(stats) + [pad], axis=0))
        half = width // 2
        tail = packed[:, width:]
        upper = jnp.concatenate([packed[:, :half], tail], axis=1)
        lower = jnp.concatenate([packed[:, half:width], tail], axis=1)
        for o in range(owners):
            cut = slice(o * GROWS, (o + 1) * GROWS)
            rs_src[l, o] = jnp.concatenate([upper[cut], lower[cut]], axis=0).astype(BF16)
        rs_start(l)

    def combine(l):
        rs_buf[l, n - 1] = rs_src[l, me]
        drain(rs_buf.at[l, pl.ds(0, n - 1)], rs_recv.at[l])
        half = width // 2
        got = rs_buf[l].astype(F32)
        upper = got[:, :GROWS, :]
        lower = got[:, GROWS:, :]
        stats = upper[:, :, half:].reshape(n * GROWS, BLK).astype(BF16)
        top = jnp.dot(stats, spread[0], preferred_element_type=F32).reshape(n, GROWS, width)
        total = jnp.dot(stats, spread[1], preferred_element_type=F32).reshape(n, GROWS, width)
        value = jnp.concatenate([upper[:, :, :half], lower[:, :, :half]], axis=2)
        factor = jnp.exp(top - jnp.max(top, axis=0, keepdims=True))
        mix = jnp.sum(value * factor, axis=0) / jnp.sum(total * factor, axis=0)
        mix = jnp.concatenate([mix, mix], axis=0).astype(BF16)
        new = gown[...] + jnp.dot(mix, wout[l], preferred_element_type=F32)[:GROWS]
        gown[...] = new
        if l + 1 < LAYERS:
            new = norm_rows(new, gg_ref[l + 1 : l + 2, :])
        ag_buf[l, me] = fold(new).astype(BF16)
        ag_start(l)

    def gathered(l):
        by_owner(lambda slots: drain(ag_buf.at[l, pl.ds(0, slots)], ag_recv.at[l]))
        got = ag_buf[l].astype(F32)
        half = width // 2
        return jnp.concatenate(
            [got[:, :GROWS].reshape(gcount, half), got[:, GROWS:].reshape(gcount, half)], axis=1
        ).astype(BF16)

    def near_part(l):
        for rb in range(2):
            for p in range(pairs):
                top, total, value = attend(l, p, rb, k_own, v_own, 0, rows)
                m_a[rb, p] = top
                l_a[rb, p] = total
                o_a[rb, p] = value

    for l in range(LAYERS):
        if l == 0:
            w_in[0].wait()
            project_global(0)
            project_local(0)
            global_part(0)
            near_part(0)
            wout_in.wait()
        else:
            w_in[l].wait()
            project_local(l)
            near_part(l)
            xa[l, rows:span, :] = gathered(l - 1)
            project_global(l)
            global_part(l)

        if l == 0:
            @pl.when(has_left)
            def _():
                seg_to_right().wait_recv()

            @pl.when(has_right)
            def _():
                seg_to_left().wait_recv()

            for side in range(2):
                for part in range(2):
                    put_marks(
                        k_far, side * span + part * BLK, marks(seg_halo[side, part : part + 1, :])
                    )

        def take_left():
            wait_left(l)
            put_keys(l, xh[l, 0:rows, :], (k_far, v_far, 0))

        def take_right():
            wait_right(l)
            put_keys(l, xh[l, rows : 2 * rows, :], (k_far, v_far, span))

        @pl.when(lax.rem(me, 2) == 0)
        def _():
            take_right()
            take_left()

        @pl.when(lax.rem(me, 2) == 1)
        def _():
            take_left()
            take_right()

        if l + 1 == LAYERS:
            only_owner(functools.partial(combine, l))

        for rb in range(2):
            for p in range(pairs):
                top_b, total_b, value_b = attend(
                    l, p, rb, k_far, v_far, rb * BLK, 4 * BLK, masked=True
                )
                top_a = m_a[rb, p]
                top = jnp.maximum(top_a, top_b)
                fa = jnp.exp(top_a - top)
                fb = jnp.exp(top_b - top)
                inv = 1.0 / (l_a[rb, p] * fa + total_b * fb)
                value = o_a[rb, p] * (fa * inv) + value_b * (fb * inv)
                mixt[rb, p * BLK : p * BLK + head_dim, :] = value[:, :BLK]
                mixt[rb, p * BLK + head_dim : (p + 1) * BLK, :] = value[:, BLK:]

            here = slice(rb * BLK, (rb + 1) * BLK)
            mix = jnp.transpose(mixt[rb].astype(BF16))
            new = stream[here, :] + jnp.dot(mix, wout[l], preferred_element_type=F32)
            if l + 1 < LAYERS:
                stream[here, :] = new
                xa[l + 1, here, :] = norm_rows(new, gl_ref[l + 1 : l + 2, :]).astype(BF16)
                send_halo(l + 1, rb)
                if rb == 0:
                    only_owner(functools.partial(combine, l))
            else:
                out_ref[here, :] = new.astype(BF16)

    gout_ref[...] = gathered(LAYERS - 1)

    @pl.when(has_right)
    def _():
        seg_to_right().wait_send()
        for l in range(LAYERS):
            for c in range(2):
                halo_to_right(l, c).wait_send()

    @pl.when(has_left)
    def _():
        seg_to_left().wait_send()
        for l in range(LAYERS):
            for c in range(2):
                halo_to_left(l, c).wait_send()

    for l in range(LAYERS):
        by_owner(lambda slots: drain(rs_src.at[l, pl.ds(0, slots)], rs_send.at[l]))
        only_owner(lambda: drain_sent(l))


def hand_on(a_ref, b_ref, a_out, b_out, a_mid, b_mid, sems):
    half = a_ref.shape[0] // 2
    first, second = pl.ds(0, half), pl.ds(half, half)
    parts = [
        (a_ref.at[first], a_mid.at[first], a_out.at[first]),
        (a_ref.at[second], a_mid.at[second], a_out.at[second]),
        (b_ref, b_mid, b_out),
    ]
    reads = [pltpu.make_async_copy(s, m, sems.at[0, i]) for i, (s, m, _) in enumerate(parts)]
    writes = [pltpu.make_async_copy(m, d, sems.at[1, i]) for i, (_, m, d) in enumerate(parts)]
    for copy in reads:
        copy.start()
    for read, write in zip(reads, writes):
        read.wait()
        write.start()
    for copy in writes:
        copy.wait()


def per_device(n, tokens, globals_in, seg_ids, table, w_qkv, w_out, gain_local, gain_global, seg_bias):
    rows, width = tokens.shape
    gcount = globals_in.shape[0]
    heads = seg_bias.shape[1]
    assert rows == 2 * BLK and gcount == BLK and heads == 8
    owners = min(n, gcount // GROWS)
    assert owners * GROWS == gcount
    span = rows + gcount
    vmem = pl.BlockSpec(memory_space=pltpu.VMEM)
    hbm = pl.BlockSpec(memory_space=pltpu.HBM)
    dma = pltpu.SemaphoreType.DMA
    V = pltpu.VMEM
    half = width // 2
    pairs, wide, head_dim = heads // 2, 2 * BLK, width // heads
    assert 2 * head_dim == BLK
    local, shared = pl.pallas_call(
        functools.partial(kernel, n, owners, heads),
        out_shape=(
            jax.ShapeDtypeStruct((rows, width), BF16),
            jax.ShapeDtypeStruct((gcount, width), BF16),
        ),
        in_specs=[hbm] * 9,
        out_specs=(vmem, vmem),
        scratch_shapes=[
            V((rows, width), BF16),
            V((gcount, width), BF16),
            V((2, BLK), jnp.int32),
            V((1, BLK), jnp.int32),
            V((LAYERS, width, 3 * width), BF16),
            V((LAYERS, width, width), BF16),
            V((LAYERS, width), F32),
            V((LAYERS, width), F32),
            V((LAYERS, heads), F32),
            V((LAYERS, span, width), BF16),
            V((LAYERS, 2 * rows, width), BF16),
            V((8, BLK), F32),
            V((2, 8, BLK), F32),
            V((LAYERS, pairs, 3, wide, wide), BF16),
            V((span, pairs * wide), BF16),
            V((pairs, BLK + ONES, span), BF16),
            V((2 * rows + gcount, pairs * wide), BF16),
            V((pairs, BLK + ONES, 2 * rows + gcount), BF16),
            V((2, BLK, wide), F32),
            V((2, BLK, width), BF16),
            V((2, pairs, head_dim, wide), F32),
            V((2, pairs, 1, wide), F32),
            V((2, pairs, 1, wide), F32),
            V((2, width, BLK), F32),
            V((rows, width), F32),
            V((gcount, width), F32),
            V((GROWS, width), F32),
            V((LAYERS, owners, 2 * GROWS, half + BLK), BF16),
            V((LAYERS, n, 2 * GROWS, half + BLK), BF16),
            V((LAYERS, owners, 2 * GROWS, half), BF16),
            dma((8 + LAYERS,)),
            dma((2,)),
            dma((2,)),
            dma((LAYERS, 2, 2)),
            dma((LAYERS, 2, 2)),
            dma((LAYERS,)),
            dma((LAYERS,)),
            dma((LAYERS,)),
            dma((LAYERS,)),
        ],
        compiler_params=pltpu.CompilerParams(
            collective_id=0, has_side_effects=True, vmem_limit_bytes=VMEM_BYTES
        ),
        name="encoder",
    )(
        tokens, globals_in, seg_ids.reshape(2, BLK), table.reshape(1, BLK),
        w_qkv, w_out, gain_local, gain_global, seg_bias,
    )
    return pl.pallas_call(
        hand_on,
        out_shape=(
            jax.ShapeDtypeStruct(local.shape, BF16),
            jax.ShapeDtypeStruct(shared.shape, BF16),
        ),
        in_specs=[hbm, hbm],
        out_specs=(hbm, hbm),
        scratch_shapes=[V(local.shape, BF16), V(shared.shape, BF16), dma((2, 3))],
        compiler_params=pltpu.CompilerParams(vmem_limit_bytes=VMEM_BYTES),
        name="hand_on",
    )(local, shared)


def solution(mesh):
    return jax.shard_map(
        functools.partial(per_device, mesh.shape["seq"]),
        mesh=mesh,
        in_specs=(
            P(("dp", "seq"), None),
            P("dp", None),
            P(("dp", "seq")),
            P("dp"),
            P(),
            P(),
            P(),
            P(),
            P(),
        ),
        out_specs=(P(("dp", "seq"), None), P("dp", None)),
        check_vma=False,
    )
```

```python
import functools

import jax
import jax.numpy as jnp
from jax import lax
from jax.experimental import pallas as pl
from jax.experimental.pallas import tpu as pltpu
from jax.sharding import PartitionSpec as P

LAYERS = 2
BLK = 128
GROWS = 8
IDS = 64
ONES = 16
VMEM_BYTES = 62 * 1024 * 1024
NEG = -1e30
F32 = jnp.float32
BF16 = jnp.bfloat16


def norm_rows(values, gain):
    average = jnp.mean(values, axis=-1, keepdims=True)
    centered = values - average
    variance = jnp.mean(centered * centered, axis=-1, keepdims=True)
    return centered * lax.rsqrt(variance + 1e-05) * gain


def three_parts(x):
    hi = x.astype(BF16).astype(F32)
    rest = x - hi
    mid = rest.astype(BF16).astype(F32)
    return hi, mid, (rest - mid).astype(BF16).astype(F32)


def fold(rows):
    half = rows.shape[1] // 2
    return jnp.concatenate([rows[:, :half], rows[:, half:]], axis=0)


def steps(first, last, body):
    if last <= 16:
        for i in range(first, last):
            body(i)
    else:
        pl.loop(first, last)(body)


def kernel(
    n, owners, heads,
    tok_hbm, glob_hbm, seg_hbm, table_hbm, wqkv_hbm, wout_hbm, gl_hbm, gg_hbm, bias_hbm,
    out_ref, gout_ref,
    tok_ref, glob_ref, seg_ref, table_ref, wqkv, wout, gl_ref, gg_ref, bias_ref,
    xa, xh, seg_own, seg_halo,
    qs, k_own, v_own, k_far, v_far, tri, spread,
    o_a, m_a, l_a, mixt, stream, gall, gown, rs_src, rs_buf, ag_buf,
    in_sem, seg_send, seg_recv, h_send, h_recv, rs_send, rs_recv, ag_send, ag_recv,
):
    rows, width = tok_ref.shape
    gcount = glob_ref.shape[0]
    head_dim = width // heads
    me = lax.axis_index("seq")
    has_left = me > 0
    has_right = me < n - 1
    left = jnp.maximum(me - 1, 0)
    right = jnp.minimum(me + 1, n - 1)

    barrier = pltpu.get_barrier_semaphore()

    each_peer = functools.partial(steps, 1, n)

    @each_peer
    def _(r):
        pl.semaphore_signal(
            barrier, inc=1, device_id={"seq": lax.rem(me + r, n)},
            device_id_type=pl.DeviceIdType.MESH,
        )

    def load(i, src, dst):
        copy = pltpu.make_async_copy(src, dst, in_sem.at[i])
        copy.start()
        return copy

    tok_in = load(0, tok_hbm, tok_ref)
    gl_in = load(1, gl_hbm, gl_ref)
    seg_in = load(2, seg_hbm, seg_ref)
    w_in = [load(3, wqkv_hbm.at[0], wqkv.at[0])]
    small_in = [
        load(4, glob_hbm, glob_ref),
        load(5, table_hbm, table_ref),
        load(6, gg_hbm, gg_ref),
        load(7, bias_hbm, bias_ref),
    ]
    wout_in = load(8, wout_hbm, wout)
    w_in += [load(8 + l, wqkv_hbm.at[l], wqkv.at[l]) for l in range(1, LAYERS)]

    pairs = heads // 2
    wide = 2 * BLK
    seg_in.wait()
    seg_own[...] = jnp.zeros(seg_own.shape, F32)
    seg_own[0:2, :] = seg_ref[...].astype(F32)

    @pl.when(jnp.logical_not(has_left))
    def _():
        seg_halo[0] = jnp.zeros(seg_halo.shape[1:], F32)
        for l in range(LAYERS):
            xh[l, 0:rows, :] = jnp.zeros((rows, width), BF16)

    @pl.when(jnp.logical_not(has_right))
    def _():
        seg_halo[1] = jnp.zeros(seg_halo.shape[1:], F32)
        for l in range(LAYERS):
            xh[l, rows : 2 * rows, :] = jnp.zeros((rows, width), BF16)

    tok_in.wait()
    gl_in.wait()
    stream[...] = tok_ref[...].astype(F32)
    xa[0, 0:rows, :] = norm_rows(stream[...], gl_ref[0:1, :]).astype(BF16)
    pl.semaphore_wait(barrier, n - 1)

    def remote(src, dst, ssem, rsem, target):
        return pltpu.make_async_remote_copy(
            src_ref=src, dst_ref=dst, send_sem=ssem, recv_sem=rsem,
            device_id={"seq": target}, device_id_type=pl.DeviceIdType.MESH,
        )

    def halo_to_right(l, c):
        piece = pl.ds(c * BLK, BLK)
        return remote(xa.at[l, piece], xh.at[l, piece], h_send.at[l, 0, c], h_recv.at[l, 0, c], right)

    def halo_to_left(l, c):
        return remote(
            xa.at[l, pl.ds(c * BLK, BLK)], xh.at[l, pl.ds(rows + c * BLK, BLK)],
            h_send.at[l, 1, c], h_recv.at[l, 1, c], left,
        )

    def seg_to_right():
        return remote(seg_own, seg_halo.at[0], seg_send.at[0], seg_recv.at[0], right)

    def seg_to_left():
        return remote(seg_own, seg_halo.at[1], seg_send.at[1], seg_recv.at[1], left)

    def send_halo(l, c):
        @pl.when(has_right)
        def _():
            halo_to_right(l, c).start()

        @pl.when(has_left)
        def _():
            halo_to_left(l, c).start()

    def wait_left(l):
        @pl.when(has_left)
        def _():
            for c in range(2):
                halo_to_right(l, c).wait_recv()

    def wait_right(l):
        @pl.when(has_right)
        def _():
            for c in range(2):
                halo_to_left(l, c).wait_recv()

    for c in range(2):
        send_halo(0, c)

    @pl.when(has_right)
    def _():
        seg_to_right().start()

    @pl.when(has_left)
    def _():
        seg_to_left().start()

    all_own = n == owners

    def only_owner(body):
        if all_own:
            body()
        else:
            pl.when(me < owners)(body)

    def rs_copy(l, target, slot):
        return remote(
            rs_src.at[l, target], rs_buf.at[l, slot], rs_send.at[l], rs_recv.at[l], target
        )

    def rs_start(l):
        def send(r):
            target = lax.rem(me + r, n)
            if all_own:
                rs_copy(l, target, r - 1).start()
            else:
                @pl.when(target < owners)
                def _():
                    rs_copy(l, target, r - 1).start()

        steps(1, n, send)

    def ag_start(l):
        def send(r):
            mine = ag_buf.at[l, me]
            remote(mine, mine, ag_send.at[l], ag_recv.at[l], lax.rem(me + r, n)).start()

        steps(1, n, send)

    def drain(ref, sem):
        pltpu.make_async_copy(ref, ref, sem).wait()

    def drain_sent(l):
        for first in range(0, n - 1, owners):
            drain(ag_buf.at[l, pl.ds(0, min(owners, n - 1 - first))], ag_send.at[l])

    def by_owner(body):
        if all_own:
            body(owners - 1)
        else:
            pl.when(me < owners)(lambda: body(owners - 1))
            pl.when(me >= owners)(lambda: body(owners))

    for copy in small_in:
        copy.wait()

    xa[0, rows : rows + gcount, :] = norm_rows(glob_ref[...].astype(F32), gg_ref[0:1, :]).astype(BF16)
    gall[...] = glob_ref[...].astype(F32)

    def take_own():
        gown[...] = gall[pl.ds(me * GROWS, GROWS), :]

    only_owner(take_own)

    lane = lax.broadcasted_iota(jnp.int32, (BLK, BLK), 1)
    lane_idf = (lane & (IDS - 1)).astype(F32)
    deep = lax.broadcasted_iota(jnp.int32, (BLK, BLK), 0)
    deep_idf = (deep & (IDS - 1)).astype(F32)
    low = deep < IDS

    def down(row):
        return jnp.transpose(jnp.broadcast_to(row, (BLK, BLK)))

    def marks(row):
        return jnp.where(down(row) == lane_idf, 1.0, 0.0).astype(F32)

    def put_marks(ref, at, value):
        for p in range(pairs):
            ref[at : at + BLK, p * wide + BLK : (p + 1) * wide] = value.astype(BF16)

    for l in range(LAYERS):
        for p in range(pairs):
            for b in range(3):
                qs[l, p, b, 0:BLK, :] = jnp.zeros((BLK, wide), BF16)

    outside = jnp.where(deep == 0, NEG, 0.0).astype(F32)
    for rb in range(2):
        row = seg_own[rb : rb + 1, :]
        put_marks(k_own, rb * BLK, marks(row))
        own = jnp.where(jnp.broadcast_to(row, (BLK, BLK)) == deep_idf, 1.0, 0.0).astype(F32)
        for l in range(LAYERS):
            for h in range(heads):
                b = jnp.broadcast_to(bias_ref[l : l + 1, h : h + 1], (BLK, BLK))
                b_hi = b.astype(BF16).astype(F32)
                qs[l, h // 2, rb, BLK:, (h % 2) * BLK : (h % 2 + 1) * BLK] = (
                    own * jnp.where(low, b_hi, b - b_hi) + outside
                ).astype(BF16)
    hidden = jnp.where(me == 0, 0.0, 1.0).astype(F32)
    g_marks = jnp.where(lane == IDS, 1.0, 0.0).astype(F32) * hidden
    put_marks(k_own, rows, g_marks)
    put_marks(k_far, rows, g_marks)
    member = jnp.broadcast_to(table_ref[...].astype(F32), (BLK, BLK)) == deep_idf
    g_side = jnp.where((low & (deep > 0) & jnp.logical_not(member)) | (deep == IDS), NEG, 0.0)
    g_side = g_side.astype(F32).astype(BF16)
    for l in range(LAYERS):
        for p in range(pairs):
            qs[l, p, 2, BLK:, 0:BLK] = g_side
            qs[l, p, 2, BLK:, BLK:] = g_side

    tr = lax.broadcasted_iota(jnp.int32, (BLK, wide), 0)
    tc = lax.broadcasted_iota(jnp.int32, (BLK, wide), 1) & (BLK - 1)
    tri[0] = jnp.where(tr >= tc, 0.0, NEG).astype(F32)
    tri[1] = jnp.where(tr <= tc, 0.0, NEG).astype(F32)
    v_own[:, BLK:, :] = jnp.ones((pairs, ONES, rows + gcount), BF16)
    v_far[:, BLK:, :] = jnp.ones((pairs, ONES, 2 * rows + gcount), BF16)

    pick = lax.broadcasted_iota(jnp.int32, (BLK, width), 0)
    start = lax.broadcasted_iota(jnp.int32, (BLK, width), 1) & (head_dim - 1)
    head_of = (lax.broadcasted_iota(jnp.int32, (BLK, width), 1) - start).astype(F32) * (1.0 / head_dim)
    pick_head = (pick & 7).astype(F32)
    for i in range(2):
        hit = (pick_head == head_of) & (pick >= 24 * i) & (pick < 24 * (i + 1))
        spread[i] = jnp.where(hit, 1.0, 0.0).astype(F32).astype(BF16)

    def put_keys(l, x, *places):
        k = jnp.dot(x, wqkv[l, :, width : 2 * width], preferred_element_type=F32).astype(BF16)
        v = jnp.dot(x, wqkv[l, :, 2 * width : 3 * width], preferred_element_type=F32).astype(BF16)
        v = jnp.transpose(v)
        for lo, size, k_ref, v_ref, at in places:
            for p in range(pairs):
                cols = slice(p * BLK, (p + 1) * BLK)
                k_ref[at : at + size, p * wide : p * wide + BLK] = k[lo : lo + size, cols]
                v_ref[p, 0:BLK, at : at + size] = v[cols, lo : lo + size]

    def put_queries(l, x, first):
        q = jnp.dot(x, wqkv[l, :, 0:width], preferred_element_type=F32)
        q = jnp.transpose((q * 0.125).astype(BF16))
        for b in range(x.shape[0] // BLK):
            for p in range(pairs):
                lanes = slice(b * BLK, (b + 1) * BLK)
                at = p * BLK
                qs[l, p, first + b, 0:head_dim, 0:BLK] = q[at : at + head_dim, lanes]
                qs[l, p, first + b, head_dim:BLK, BLK:] = q[at + head_dim : at + BLK, lanes]

    def project_local(l):
        x = xa[l, 0:rows, :]
        put_queries(l, x, 0)
        put_keys(l, x, (0, rows, k_own, v_own, 0))

    def project_global(l):
        x = xa[l, rows : rows + gcount, :]
        put_queries(l, x, 2)
        put_keys(l, x, (0, gcount, k_own, v_own, rows), (0, gcount, k_far, v_far, rows))

    def attend(l, p, rb, k_ref, v_ref, k0, count, masked=False):
        s = jnp.dot(
            k_ref[k0 : k0 + count, p * wide : (p + 1) * wide], qs[l, p, rb],
            preferred_element_type=F32,
        )
        if masked:
            s = jnp.concatenate(
                [s[:BLK] + tri[0], s[BLK : count - BLK], s[count - BLK :] + tri[1]], axis=0
            )
        top = jnp.max(s, axis=0, keepdims=True)
        probs = jnp.exp(s - top).astype(BF16)
        mixed = jnp.dot(v_ref[p, :, k0 : k0 + count], probs, preferred_element_type=F32)
        value = jnp.concatenate([mixed[:head_dim, :BLK], mixed[head_dim:BLK, BLK:]], axis=1)
        return top, mixed[BLK : BLK + 1], value

    span = rows + gcount

    def global_part(l):
        tops, totals, parts = [], [], []
        for p in range(pairs):
            top, total, value = attend(l, p, 2, k_own, v_own, 0, span)
            for lanes in (slice(0, BLK), slice(BLK, wide)):
                tops.append(top[:, lanes])
                totals.append(total[:, lanes])
                parts.append(value[:, lanes])
        stats = three_parts(jnp.concatenate(tops, axis=0)) + three_parts(jnp.concatenate(totals, axis=0))
        pad = jnp.zeros((BLK - 6 * heads, BLK), F32)
        packed = jnp.transpose(jnp.concatenate(parts + list(stats) + [pad], axis=0))
        half = width // 2
        tail = packed[:, width:]
        upper = jnp.concatenate([packed[:, :half], tail], axis=1)
        lower = jnp.concatenate([packed[:, half:width], tail], axis=1)
        for o in range(owners):
            cut = slice(o * GROWS, (o + 1) * GROWS)
            rs_src[l, o] = jnp.concatenate([upper[cut], lower[cut]], axis=0).astype(BF16)
        rs_start(l)

    def combine(l):
        rs_buf[l, n - 1] = rs_src[l, me]
        drain(rs_buf.at[l, pl.ds(0, n - 1)], rs_recv.at[l])
        half = width // 2
        got = rs_buf[l].astype(F32)
        upper = got[:, :GROWS, :]
        lower = got[:, GROWS:, :]
        stats = upper[:, :, half:].reshape(n * GROWS, BLK).astype(BF16)
        top = jnp.dot(stats, spread[0], preferred_element_type=F32).reshape(n, GROWS, width)
        total = jnp.dot(stats, spread[1], preferred_element_type=F32).reshape(n, GROWS, width)
        value = jnp.concatenate([upper[:, :, :half], lower[:, :, :half]], axis=2)
        factor = jnp.exp(top - jnp.max(top, axis=0, keepdims=True))
        mix = jnp.sum(value * factor, axis=0) / jnp.sum(total * factor, axis=0)
        mix = jnp.concatenate([mix, mix], axis=0).astype(BF16)
        new = gown[...] + jnp.dot(mix, wout[l], preferred_element_type=F32)[:GROWS]
        gown[...] = new
        if l + 1 < LAYERS:
            new = norm_rows(new, gg_ref[l + 1 : l + 2, :])
        ag_buf[l, me] = fold(new).astype(BF16)
        ag_start(l)

    def gathered(l):
        by_owner(lambda slots: drain(ag_buf.at[l, pl.ds(0, slots)], ag_recv.at[l]))
        got = ag_buf[l].astype(F32)
        half = width // 2
        return jnp.concatenate(
            [got[:, :GROWS].reshape(gcount, half), got[:, GROWS:].reshape(gcount, half)], axis=1
        ).astype(BF16)

    def near_part(l):
        for rb in range(2):
            for p in range(pairs):
                top, total, value = attend(l, p, rb, k_own, v_own, 0, rows)
                m_a[rb, p] = top
                l_a[rb, p] = total
                o_a[rb, p] = value

    for l in range(LAYERS):
        if l == 0:
            w_in[0].wait()
            put_queries(0, xa[0], 0)
            put_keys(0, xa[0], (0, span, k_own, v_own, 0), (rows, gcount, k_far, v_far, rows))
            global_part(0)
            near_part(0)
            wout_in.wait()
        else:
            w_in[l].wait()
            project_local(l)
            near_part(l)
            xa[l, rows:span, :] = gathered(l - 1)
            project_global(l)
            global_part(l)

        if l == 0:
            @pl.when(has_left)
            def _():
                seg_to_right().wait_recv()

            @pl.when(has_right)
            def _():
                seg_to_left().wait_recv()

            for side in range(2):
                for part in range(2):
                    put_marks(
                        k_far, side * span + part * BLK, marks(seg_halo[side, part : part + 1, :])
                    )

        wait_left(l)
        wait_right(l)
        put_keys(l, xh[l], (0, rows, k_far, v_far, 0), (rows, rows, k_far, v_far, span))
        only_owner(functools.partial(combine, l))

        for rb in range(2):
            for p in range(pairs):
                top_b, total_b, value_b = attend(
                    l, p, rb, k_far, v_far, rb * BLK, 4 * BLK, masked=True
                )
                top_a = m_a[rb, p]
                top = jnp.maximum(top_a, top_b)
                fa = jnp.exp(top_a - top)
                fb = jnp.exp(top_b - top)
                inv = 1.0 / (l_a[rb, p] * fa + total_b * fb)
                value = o_a[rb, p] * (fa * inv) + value_b * (fb * inv)
                mixt[rb, p * BLK : p * BLK + head_dim, :] = value[:, :BLK]
                mixt[rb, p * BLK + head_dim : (p + 1) * BLK, :] = value[:, BLK:]

            here = slice(rb * BLK, (rb + 1) * BLK)
            mix = jnp.transpose(mixt[rb].astype(BF16))
            new = stream[here, :] + jnp.dot(mix, wout[l], preferred_element_type=F32)
            if l + 1 < LAYERS:
                stream[here, :] = new
                xa[l + 1, here, :] = norm_rows(new, gl_ref[l + 1 : l + 2, :]).astype(BF16)
                send_halo(l + 1, rb)
            else:
                out_ref[here, :] = new.astype(BF16)

    gout_ref[...] = gathered(LAYERS - 1)

    @pl.when(has_right)
    def _():
        seg_to_right().wait_send()
        for l in range(LAYERS):
            for c in range(2):
                halo_to_right(l, c).wait_send()

    @pl.when(has_left)
    def _():
        seg_to_left().wait_send()
        for l in range(LAYERS):
            for c in range(2):
                halo_to_left(l, c).wait_send()

    for l in range(LAYERS):
        by_owner(lambda slots: drain(rs_src.at[l, pl.ds(0, slots)], rs_send.at[l]))
        only_owner(lambda: drain_sent(l))


def hand_on(a_ref, b_ref, a_out, b_out, a_mid, b_mid, sems):
    half = a_ref.shape[0] // 2
    first, second = pl.ds(0, half), pl.ds(half, half)
    parts = [
        (a_ref.at[first], a_mid.at[first], a_out.at[first]),
        (a_ref.at[second], a_mid.at[second], a_out.at[second]),
        (b_ref, b_mid, b_out),
    ]
    reads = [pltpu.make_async_copy(s, m, sems.at[0, i]) for i, (s, m, _) in enumerate(parts)]
    writes = [pltpu.make_async_copy(m, d, sems.at[1, i]) for i, (_, m, d) in enumerate(parts)]
    for copy in reads:
        copy.start()
    for read, write in zip(reads, writes):
        read.wait()
        write.start()
    for copy in writes:
        copy.wait()


def per_device(n, tokens, globals_in, seg_ids, table, w_qkv, w_out, gain_local, gain_global, seg_bias):
    rows, width = tokens.shape
    gcount = globals_in.shape[0]
    heads = seg_bias.shape[1]
    assert rows == 2 * BLK and gcount == BLK and heads == 8
    owners = min(n, gcount // GROWS)
    assert owners * GROWS == gcount
    span = rows + gcount
    vmem = pl.BlockSpec(memory_space=pltpu.VMEM)
    hbm = pl.BlockSpec(memory_space=pltpu.HBM)
    dma = pltpu.SemaphoreType.DMA
    V = pltpu.VMEM
    half = width // 2
    pairs, wide, head_dim = heads // 2, 2 * BLK, width // heads
    assert 2 * head_dim == BLK
    local, shared = pl.pallas_call(
        functools.partial(kernel, n, owners, heads),
        out_shape=(
            jax.ShapeDtypeStruct((rows, width), BF16),
            jax.ShapeDtypeStruct((gcount, width), BF16),
        ),
        in_specs=[hbm] * 9,
        out_specs=(vmem, vmem),
        scratch_shapes=[
            V((rows, width), BF16),
            V((gcount, width), BF16),
            V((2, BLK), jnp.int32),
            V((1, BLK), jnp.int32),
            V((LAYERS, width, 3 * width), BF16),
            V((LAYERS, width, width), BF16),
            V((LAYERS, width), F32),
            V((LAYERS, width), F32),
            V((LAYERS, heads), F32),
            V((LAYERS, span, width), BF16),
            V((LAYERS, 2 * rows, width), BF16),
            V((8, BLK), F32),
            V((2, 8, BLK), F32),
            V((LAYERS, pairs, 3, wide, wide), BF16),
            V((span, pairs * wide), BF16),
            V((pairs, BLK + ONES, span), BF16),
            V((2 * rows + gcount, pairs * wide), BF16),
            V((pairs, BLK + ONES, 2 * rows + gcount), BF16),
            V((2, BLK, wide), F32),
            V((2, BLK, width), BF16),
            V((2, pairs, head_dim, wide), F32),
            V((2, pairs, 1, wide), F32),
            V((2, pairs, 1, wide), F32),
            V((2, width, BLK), F32),
            V((rows, width), F32),
            V((gcount, width), F32),
            V((GROWS, width), F32),
            V((LAYERS, owners, 2 * GROWS, half + BLK), BF16),
            V((LAYERS, n, 2 * GROWS, half + BLK), BF16),
            V((LAYERS, owners, 2 * GROWS, half), BF16),
            dma((8 + LAYERS,)),
            dma((2,)),
            dma((2,)),
            dma((LAYERS, 2, 2)),
            dma((LAYERS, 2, 2)),
            dma((LAYERS,)),
            dma((LAYERS,)),
            dma((LAYERS,)),
            dma((LAYERS,)),
        ],
        compiler_params=pltpu.CompilerParams(
            collective_id=0, has_side_effects=True, vmem_limit_bytes=VMEM_BYTES
        ),
        name="encoder",
    )(
        tokens, globals_in, seg_ids.reshape(2, BLK), table.reshape(1, BLK),
        w_qkv, w_out, gain_local, gain_global, seg_bias,
    )
    return pl.pallas_call(
        hand_on,
        out_shape=(
            jax.ShapeDtypeStruct(local.shape, BF16),
            jax.ShapeDtypeStruct(shared.shape, BF16),
        ),
        in_specs=[hbm, hbm],
        out_specs=(hbm, hbm),
        scratch_shapes=[V(local.shape, BF16), V(shared.shape, BF16), dma((2, 3))],
        compiler_params=pltpu.CompilerParams(vmem_limit_bytes=VMEM_BYTES),
        name="hand_on",
    )(local, shared)


def solution(mesh):
    return jax.shard_map(
        functools.partial(per_device, mesh.shape["seq"]),
        mesh=mesh,
        in_specs=(
            P(("dp", "seq"), None),
            P("dp", None),
            P(("dp", "seq")),
            P("dp"),
            P(),
            P(),
            P(),
            P(),
            P(),
        ),
        out_specs=(P(("dp", "seq"), None), P("dp", None)),
        check_vma=False,
    )
```
